32 devices in a mesh: dp: 8 (over z, y), tensor: 4 (over x, core).
Axes of the slice: x: 2, y: 2, z: 4, core: 2. Of those that a mesh axis runs over, the one named last changes fastest.
Arguments:
- enc_input: bfloat16 [8192, 768], P(('dp', 'tensor')), may hold values from -6 to 6
- dec_input: bfloat16 [2048, 768], P(('dp', 'tensor')), may hold values from -6 to 6
- segment_ids: int32 [8, 1024], P('dp'), may hold values from 0 to 7, never falling along the last dimension, each value on 1 to 512 neighbouring positions
- retrieval: int32 [8, 256, 12, 128], P('dp', None, 'tensor'), may hold values from 0 to 1023
- att_in: bfloat16 [9, 768, 768], P(None, None, 'tensor'), may hold values from -0.21875 to 0.21875
- att_in_bias: bfloat16 [6, 768], P(None, 'tensor'), may hold values from -3 to 3
- att_out: bfloat16 [3, 768, 768], P(None, None, 'tensor'), may hold values from -0.875 to 0.875
- att_out_bias: bfloat16 [3, 768], replicated, may hold values from -3 to 3
- ffn_in: bfloat16 [2, 768, 3072], P(None, None, 'tensor'), may hold values from -0.21875 to 0.21875
- ffn_in_bias: bfloat16 [2, 3072], P(None, 'tensor'), may hold values from -3 to 3
- ffn_out: bfloat16 [2, 768, 3072], P(None, None, 'tensor'), may hold values from -0.109375 to 0.109375
- ffn_out_bias: bfloat16 [2, 768], replicated, may hold values from -3 to 3
- ln_gain: bfloat16 [5, 768], replicated, may hold values from 0.5 to 1.5
- ln_bias: bfloat16 [5, 768], replicated, may hold values from -3 to 3
- d_out: bfloat16 [2048, 768], P(('dp', 'tensor')), may hold values from -6 to 6
Outputs:
- dec_output: bfloat16 [2048, 768], P(('dp', 'tensor'))
- enc_input_grad: float32 [8192, 768], P(('dp', 'tensor'))
- dec_input_grad: float32 [2048, 768], P(('dp', 'tensor'))
- att_in_grad: float32 [9, 768, 768], P(None, 'dp', 'tensor')
- att_in_bias_grad: float32 [6, 768], replicated
- att_out_grad: float32 [3, 768, 768], P(None, 'dp', 'tensor')
- att_out_bias_grad: float32 [3, 768], replicated
- ffn_in_grad: float32 [2, 768, 3072], P(None, 'dp', 'tensor')
- ffn_in_bias_grad: float32 [2, 3072], replicated
- ffn_out_grad: float32 [2, 768, 3072], P(None, 'dp', 'tensor')
- ffn_out_bias_grad: float32 [2, 768], replicated
- ln_gain_grad: float32 [5, 768], replicated
- ln_bias_grad: float32 [5, 768], replicated
- rms_values: float32 [7], replicated
The draws below stay inside these ranges and needn't reach their ends.
Inputs may be any that keep to these rules, and one draw needn't show every extreme that they name: `segment_ids`: along a sequence the ids never fall; every document has 1 to 512 tokens and some document has exactly 512. `retrieval`: each entry is a position among the encoder tokens of the same sequence; entries of one token and head may repeat.
All inputs are finite; a program needn't handle non-finite values.
Results may differ from the reference program's by a relative error of at most 0.025.
Values may be sent and summed in bfloat16 or wider, within the bound.
A program may use at most 192 MiB of HBM per device.

```python
import math
import jax
import jax.numpy as jnp
import numpy as np
from jax import lax

D = 768
HEADS = 12
HEAD_DIM = 64
FF = 3072
S_ENC = 1024
T_DEC = 256
TOPK = 128
DOCS = 8
DOC_MOST = 512
SEQS = 8
ENC_TOKENS = 8192
DEC_TOKENS = 2048


def place_ends(values, rng, low, top_value):
    longest = values.shape.index(max(values.shape))
    spots = []
    for shift in (0, 1):
        where = [jax.random.randint(jax.random.fold_in(rng, axis), (), 0, length) for axis, length in enumerate(values.shape)]
        where[longest] = (where[longest] + shift) % values.shape[longest]
        spots.append(tuple(where))
    return values.at[spots[0]].set(low).at[spots[1]].set(top_value)


def with_spikes(values, rng, source, target, shards_of, factor):
    def block_of(position):
        return (jnp.arange(values.shape[position]) // (values.shape[position] // shards_of)).reshape((-1,) + (1,) * (values.ndim - 1 - position))

    near = jax.random.permutation(rng, shards_of)[block_of(target)]
    far = (block_of(target) + shards_of // 2) % shards_of
    return jnp.where((block_of(source) == near) | (block_of(source) == far), factor * values, values)


def level_of(own_key, shape, split, least, top_value):
    def one(dim, blocks):
        steps = jax.random.uniform(jax.random.fold_in(jax.random.fold_in(own_key, 6), dim), (blocks,), jnp.float32, least / len(split), top_value / len(split))
        return jnp.repeat(jnp.exp(steps), shape[dim] // blocks).reshape((-1,) + (1,) * (len(shape) - dim - 1))

    factor_of = one(*split[0])
    for cut in split[1:]:
        factor_of = factor_of * one(*cut)
    return factor_of


def profile(count, total, reach, lean):
    weights = [(1 << 20) // math.isqrt(grade ** lean) + 1 for grade in range(2, count + 1)]
    surplus, holding = total - reach - (count - 1), [1] * (count - 1)
    while surplus > 0:
        candidates = [i for i in range(count - 1) if holding[i] < reach]
        pool, remaining = sum([weights[i] for i in candidates]), surplus
        for i in candidates:
            more = min(reach - holding[i], max(1, remaining * weights[i] // pool), surplus)
            holding[i] = holding[i] + more
            surplus = surplus - more
    return np.array([reach] + holding)


def uneven_parts(stream_key, number_of, total, most, skew):
    if number_of == 2:
        one = jax.random.randint(stream_key, (), max(1, total - most), min(most, total - 1) + 1)
        return jnp.stack([one, total - one])
    lengths = jnp.asarray(profile(number_of, total, most, skew), jnp.int32)
    pairs = (number_of - 1) // 2
    source_of, sink = lengths[1:1 + 2 * pairs:2], lengths[2:2 + 2 * pairs:2]
    margin = jnp.minimum(source_of - 1, most - sink)
    moved = jax.random.randint(jax.random.fold_in(stream_key, 1), (pairs,), 0, 1 << 20) % (margin + 1)
    lengths = lengths.at[1:1 + 2 * pairs:2].set(source_of - moved).at[2:2 + 2 * pairs:2].set(sink + moved)
    return lengths[jax.random.permutation(jax.random.fold_in(stream_key, 2), number_of)]


def gaussian(key, dims, scale, bound, cuts=(), kind=jnp.bfloat16):
    level = level_of(key, dims, cuts, -0.22, 0.18) if cuts else 1.0
    entries = jax.random.normal(key, dims, jnp.float32) * scale * level
    return jnp.minimum(jnp.maximum(entries, -bound), bound).astype(kind)


def gaussian_with(rng, extent, scale, reach, shards, heavy, held_as=jnp.bfloat16):
    values = scale * jax.random.normal(rng, extent, jnp.float32)
    if shards:
        values = values * level_of(rng, extent, shards, -0.22, 0.18)
    return jnp.clip(with_spikes(values, jax.random.fold_in(rng, 3), *heavy), -reach, reach).astype(held_as)


def setup_inputs(seed: int = 0) -> dict:
    key_list = jax.random.split(jax.random.key(seed), 16)
    return {
        "enc_input": gaussian(key_list[0], (ENC_TOKENS, D), 1.0, 6.0, ((0, 32),)),
        "dec_input": gaussian(key_list[1], (DEC_TOKENS, D), 1.0, 6.0, ((0, 32),)),
        "segment_ids": jax.vmap(lambda own: jnp.searchsorted(jnp.cumsum(uneven_parts(own, DOCS, S_ENC, DOC_MOST, 2)), jnp.arange(S_ENC), side="right"))(jax.random.split(key_list[2], SEQS)).reshape((SEQS, S_ENC)).astype(jnp.int32),
        "retrieval": place_ends(jax.random.randint(key_list[3], (SEQS, T_DEC, HEADS, TOPK), 0, S_ENC), jax.random.fold_in(key_list[3], 1), 0, S_ENC - 1).astype(jnp.int32),
        "att_in": gaussian(key_list[4], (9, D, D), D ** -0.5, 0.21875, ((2, 4),)),
        "att_in_bias": gaussian(key_list[5], (6, D), 0.5, 3.0, ((1, 4),)),
        "att_out": gaussian(key_list[6], (3, D, D), (D // 16) ** -0.5, 0.875, ((2, 4),)),
        "att_out_bias": gaussian(key_list[7], (3, D), 0.5, 3.0),
        "ffn_in": gaussian(key_list[8], (2, D, FF), D ** -0.5, 0.21875, ((2, 4),)),
        "ffn_in_bias": gaussian(key_list[9], (2, FF), 0.5, 3.0, ((1, 4),)),
        "ffn_out": gaussian(key_list[10], (2, D, FF), FF ** -0.5, 0.109375, ((2, 4),)),
        "ffn_out_bias": gaussian(key_list[11], (2, D), 0.5, 3.0),
        "ln_gain": jnp.clip(1.0 + 0.1 * jax.random.normal(key_list[12], (5, D), jnp.float32), 0.5, 1.5).astype(jnp.bfloat16),
        "ln_bias": gaussian(key_list[13], (5, D), 0.5, 3.0),
        "d_out": gaussian_with(key_list[14], (DEC_TOKENS, D), 1.0, 6.0, ((0, 32),), (0, 1, 32, 2.75)),
    }


highest = lax.Precision.HIGHEST

@jax.custom_vjp
def low(v):
    return lax.optimization_barrier(v.astype(jnp.bfloat16)).astype(jnp.float32)

@jax.custom_vjp
def low_back(v):
    return v

def low_keep(v):
    return (low(v), None)

def low_pass(kept, grad):
    return (grad,)

def back_keep(v):
    return (v, None)

def back_low(kept, grad):
    return (low(grad),)
low.defvjp(low_keep, low_pass)
low_back.defvjp(back_keep, back_low)

def product(left, right):
    return jnp.dot(left, right, precision=highest, preferred_element_type=jnp.float32)

def layer_norm(values, gain, shift):
    center = values - lax.optimization_barrier(jnp.mean(values, axis=-1, keepdims=True))
    spread = lax.optimization_barrier(jnp.mean(center * center, axis=-1, keepdims=True))
    return center * lax.rsqrt(spread + 1e-05) * gain + shift

def attention(source, memory, index, weights, params):
    att_in, att_in_bias, att_out, att_out_bias = (params[0], params[1], params[2], params[3])
    rows = source.shape[0]
    width = memory.shape[0]
    queries = low(low_back(product(source, att_in[3 * index]) + att_in_bias[2 * index])).reshape(rows, HEADS, HEAD_DIM)
    key_rows = low(low_back(product(memory, att_in[3 * index + 1]))).reshape(width, HEADS, HEAD_DIM)
    values = low(low_back(product(memory, att_in[3 * index + 2]) + att_in_bias[2 * index + 1])).reshape(width, HEADS, HEAD_DIM)
    scores = low_back(jnp.einsum('qhe,khe->hqk', queries, key_rows, precision=highest) * 0.125)
    masked = jnp.where(weights > 0, scores, -1e+30)
    top = lax.optimization_barrier(jnp.max(masked, axis=-1, keepdims=True))
    expo = weights * jnp.exp(scores - top)
    probs = low(expo / lax.optimization_barrier(jnp.sum(expo, axis=-1, keepdims=True)))
    mixed = jnp.einsum('hqk,khe->qhe', probs, values, precision=highest).reshape(rows, D)
    mixed = low(low_back(mixed))
    return low_back(product(mixed, att_out[index].T)) + att_out_bias[index]

def feed(source, index, params):
    ffn_in, ffn_in_bias, ffn_out, ffn_out_bias = (params[4], params[5], params[6], params[7])
    before = low_back(product(source, ffn_in[index]) + ffn_in_bias[index])
    active = low(jax.nn.gelu(before, approximate=False))
    return low_back(product(active, ffn_out[index].T)) + ffn_out_bias[index]

def forward(params, enc_x, dec_x, same, causal, counts):
    ln_gain, ln_bias = (params[8], params[9])
    branch0 = attention(enc_x, enc_x, 0, same, params)
    outer1 = layer_norm(enc_x + branch0, ln_gain[0], ln_bias[0])
    branch1 = feed(low(outer1), 0, params)
    outer2 = layer_norm(outer1 + branch1, ln_gain[1], ln_bias[1])
    memory = low(outer2)
    branch2 = attention(dec_x, dec_x, 1, causal, params)
    outer3 = layer_norm(dec_x + branch2, ln_gain[2], ln_bias[2])
    branch3 = attention(low(outer3), memory, 2, counts, params)
    outer4 = layer_norm(outer3 + branch3, ln_gain[3], ln_bias[3])
    branch4 = feed(low(outer4), 1, params)
    outer5 = layer_norm(outer4 + branch4, ln_gain[4], ln_bias[4])
    squares = jnp.stack([jnp.sum(branch0 * branch0), jnp.sum(branch1 * branch1), jnp.sum(branch2 * branch2), jnp.sum(branch3 * branch3), jnp.sum(branch4 * branch4), jnp.sum(outer2 * outer2), jnp.sum(outer5 * outer5)])
    return (outer5, squares)

def reference(enc_input, dec_input, segment_ids, retrieval, att_in, att_in_bias, att_out, att_out_bias, ffn_in, ffn_in_bias, ffn_out, ffn_out_bias, ln_gain, ln_bias, d_out):
    params = tuple((weight.astype(jnp.float32) for weight in (att_in, att_in_bias, att_out, att_out_bias, ffn_in, ffn_in_bias, ffn_out, ffn_out_bias, ln_gain, ln_bias)))
    enc_all = enc_input.astype(jnp.float32).reshape(SEQS, S_ENC, D)
    dec_all = dec_input.astype(jnp.float32).reshape(SEQS, T_DEC, D)
    cot_all = d_out.astype(jnp.float32).reshape(SEQS, T_DEC, D)
    row_index = lax.broadcasted_iota(jnp.int32, (T_DEC, T_DEC), 0)
    col_index = lax.broadcasted_iota(jnp.int32, (T_DEC, T_DEC), 1)
    causal = (row_index >= col_index).astype(jnp.float32)[None]

    def one_sequence(carry, inputs):
        grads, squares = carry
        enc_x, dec_x, segs, picks, cotangent = inputs
        same = (segs[:, None] == segs[None, :]).astype(jnp.float32)[None]
        step_index = lax.broadcasted_iota(jnp.int32, picks.shape, 0)
        head_index = lax.broadcasted_iota(jnp.int32, picks.shape, 1)
        counts = jnp.zeros((HEADS, T_DEC, S_ENC), jnp.float32).at[head_index, step_index, picks].add(1.0)

        def run(params_in, enc_in, dec_in):
            return forward(params_in, enc_in, dec_in, same, causal, counts)
        output, pullback, sums = jax.vjp(run, params, enc_x, dec_x, has_aux=True)
        grad_params, grad_enc, grad_dec = pullback(cotangent)
        grads = jax.tree.map(jnp.add, grads, grad_params)
        return ((grads, squares + sums), (output.astype(jnp.bfloat16), grad_enc, grad_dec))
    start = (jax.tree.map(jnp.zeros_like, params), jnp.zeros((7,), jnp.float32))
    (grads, squares), (outputs, enc_grads, dec_grads) = lax.scan(one_sequence, start, (enc_all, dec_all, segment_ids, retrieval, cot_all))
    enc_count = 1.0 * ENC_TOKENS * D
    dec_count = 1.0 * DEC_TOKENS * D
    totals = jnp.array([enc_count, enc_count, dec_count, dec_count, dec_count, enc_count, dec_count], dtype=jnp.float32)
    rms_values = jnp.sqrt(squares / totals)
    return (outputs.reshape(DEC_TOKENS, D), enc_grads.reshape(ENC_TOKENS, D), dec_grads.reshape(DEC_TOKENS, D), grads[0], grads[1], grads[2], grads[3], grads[4], grads[5], grads[6], grads[7], grads[8], grads[9], rms_values)
```

```python
import functools
from types import SimpleNamespace
from typing import Any, NamedTuple

import jax
import jax.numpy as jnp
from jax import lax
from jax.experimental import pallas as pl
from jax.experimental.pallas import tpu as pltpu
from jax.sharding import PartitionSpec as P

HEAD = 64
EPS = 1e-05
NEG = -1e30
MESH = pl.DeviceIdType.MESH
DP, TENSOR = "dp", "tensor"
PROBS, ALL_GRADS = "probs", "grads"
F32 = jnp.float32
BF16 = jnp.bfloat16

ROW_ATT_OUT_BIAS = 0
ROW_FFN_OUT_BIAS = 3
ROW_GAIN = 5
ROW_SHIFT = 10
ROW_SQUARE = 15
ROW_FFN_IN_BIAS = 24
SUM_ROWS = 32
BIAS_ROWS = 8

ATT, FFN_IN, FFN_OUT = range(3)
GRADS = (
    (FFN_OUT, 1, (1, 2, 4)),
    (FFN_IN, 1, (2, 1, 4)),
    (ATT, 2, (1, 2, 4)),
    (ATT, 1, (2, 1, 4)),
    (FFN_OUT, 0, (1, 2, 4)),
    (FFN_IN, 0, (2, 1, 4)),
    (ATT, 0, (2, 1, 4)),
)
SLOTS = 4


def mm(left, right):
    return jnp.dot(left, right, preferred_element_type=F32)


def mm_nt(left, right):
    return lax.dot_general(left, right, (((1,), (1,)), ((), ())), preferred_element_type=F32)


def mm_tn(left, right):
    return lax.dot_general(left, right, (((0,), (0,)), ((), ())), preferred_element_type=F32)


def bit_of(value, bit):
    return lax.rem(lax.div(value, jnp.int32(bit)), jnp.int32(2))


def flipped(value, bit):
    return value + bit - 2 * bit * bit_of(value, bit)


def column_sum(values):
    return jnp.sum(values, axis=0, keepdims=True)


class Inputs(NamedTuple):
    enc_input: Any
    dec_input: Any
    segment_ids: Any
    retrieval: Any
    att_in: Any
    att_in_bias: Any
    att_out: Any
    att_out_bias: Any
    ffn_in: Any
    ffn_in_bias: Any
    ffn_out: Any
    ffn_out_bias: Any
    ln_gain: Any
    ln_bias: Any
    d_out: Any


IN_HBM = Inputs(
    enc_input=True,
    dec_input=True,
    segment_ids=False,
    retrieval=True,
    att_in=True,
    att_in_bias=False,
    att_out=True,
    att_out_bias=False,
    ffn_in=True,
    ffn_in_bias=False,
    ffn_out=True,
    ffn_out_bias=False,
    ln_gain=False,
    ln_bias=False,
    d_out=True,
)


class Plan:
    def __init__(self, args, n_dp):
        self.D = D = args.enc_input.shape[1]
        self.CE = CE = args.enc_input.shape[0]
        self.HD = HD = args.dec_input.shape[0]
        self.HE = HE = CE // 2
        self.CD = 2 * HD
        self.R = R = 4 * CE
        self.S = S = 4 * HD
        self.A = A = args.att_in.shape[1]
        self.heads = heads = A // HEAD
        self.F = F = args.ffn_in.shape[2]
        self.picks = args.retrieval.shape[3]
        self.inside = n_dp == 8
        self.block = D // 8
        self.scratch = {}
        self.n_sems = 0
        self.at = SimpleNamespace()

        wide = ((R, D), BF16)
        short = ((S, D), BF16)
        enc_heads = ((R, A), BF16)
        dec_heads = ((S, A), BF16)
        enc_float = ((4, HE, D), F32)
        dec_float = ((2, HD, D), F32)
        enc_half = ((4, HE, D), BF16)
        dec_half = ((2, HD, D), BF16)
        enc_column = ((4, HE, 1), F32)
        dec_column = ((2, HD, 1), F32)
        stacked = ((heads * CE, A), BF16)
        self.vmem(
            ATI=((9, A, D), BF16),
            ATO=((3, A, D), BF16),
            FFI=((D, F), BF16),
            FFO=((D, F), BF16),
            RET=((heads, S, self.picks), jnp.int32),
        )
        self.vmem(X=wide, H1=wide, MEM=wide, E2=wide)
        self.vmem(DX=short, G1=short, G2=short, E5=short, E4=short, E3=short)
        self.vmem(DOU=dec_half, G3S=dec_half)
        self.vmem(Q=enc_heads, K=enc_heads, V=enc_heads, O=enc_heads, UP=enc_heads)
        self.vmem(K2=enc_heads, V2=enc_heads)
        self.vmem(QD=dec_heads, KD=dec_heads, VD=dec_heads, OD=dec_heads, UPD=dec_heads)
        self.vmem(Q2=dec_heads, O2=dec_heads, D2=dec_heads)
        self.vmem(DK=((R, A), F32), DV=((R, A), F32))
        self.vmem(BIG=((3, heads * CE, R), BF16), PD=((heads * S, S), BF16), QS=stacked, DOS=stacked)
        self.vmem(ACT0=((R, F), BF16), GP0=((R, F), BF16), ACT1=((S, F), BF16), GP1=((S, F), BF16))
        self.vmem(XH0=enc_float, XH1=enc_float, RES=enc_float)
        self.vmem(XH2=dec_float, XH3=dec_float, XH4=dec_float, RESD=dec_float)
        self.vmem(RS0=enc_column, RS1=enc_column, RS2=dec_column, RS3=dec_column, RS4=dec_column)
        self.vmem(SEGR=((1, R), F32), SEGC=((R, 1), F32), T=((D, R), BF16))
        self.vmem(OWN=((HE, D), F32), OWND=((HD, D), F32))
        self.vmem(PR=enc_half, PS=enc_half, XS=enc_half, XR=((2, 4, HE, D), BF16))
        self.vmem(PRD=dec_half, PSD=dec_half, XSD=dec_half, XRD=((2, 2, HD, D), BF16))
        self.vmem(GR=((SLOTS, 8, self.block, D), BF16))
        if self.inside:
            self.vmem(
                R1=((SLOTS, 4, self.block, D), BF16),
                R2=((SLOTS, 2, self.block, D), BF16),
                R3=((SLOTS, 1, self.block, D), BF16),
                SUMR=((5, SUM_ROWS, D), F32),
                BIAR=((5, 4 * BIAS_ROWS, 256), F32),
            )
        self.vmem(SUM=((SUM_ROWS, D), F32), BIA=((4 * BIAS_ROWS, 256), F32))
        self.vmem(GAIN=((5, D), F32), SHIFT=((5, D), F32))
        self.vmem(AIB=((6, A), F32), AOB=((3, D), F32), FIB=((2, F), F32), FOB=((2, D), F32))
        self.sem(load=8, own=4, ag=24, pst=2, enc=24, dec=12)
        self.sem(H1=8, MEM=8, E2=8, E1=8, G1=4, G2=4, E5=4, E4=4, E3=4)
        self.sem(grad=42, sum=20)

    def vmem(self, **buffers):
        for name, (shape, dtype) in buffers.items():
            self.scratch[name] = pltpu.VMEM(shape, dtype)

    def sem(self, **counts):
        for name, count in counts.items():
            setattr(self.at, name, self.n_sems)
            self.n_sems += count


class Outputs(NamedTuple):
    dec_output: Any
    enc_grad: Any
    dec_grad: Any
    sums: Any
    biases: Any
    probs: Any
    grads: Any = None
    att_in: Any = None
    att_out: Any = None
    ffn_in: Any = None
    ffn_out: Any = None


def kernel(p, made, *refs):
    n_in = len(Inputs._fields)
    ins = Inputs(*refs[:n_in])
    outs = Outputs(*[None if index is None else refs[n_in + index] for index in made])
    n_out = sum(index is not None for index in made)
    b = SimpleNamespace(**dict(zip(p.scratch, refs[n_in + n_out : -2])))
    sems, free = refs[-2:]
    b.CNT, b.DS = b.BIG.at[1], b.BIG.at[2]
    D, A, F, R, S, CE, HE, CD, HD = p.D, p.A, p.F, p.R, p.S, p.CE, p.HE, p.CD, p.HD
    heads, at = p.heads, p.at

    t = lax.axis_index(TENSOR)
    dp = lax.axis_index(DP)
    x, c = lax.div(t, jnp.int32(2)), lax.rem(t, jnp.int32(2))
    pair = (dp, t + 1 - 2 * c)
    across = (dp, t + 2 - 4 * x)

    def sem(base, index):
        return sems.at[base + index]

    def remote(src, dst, base, index, target):
        return pltpu.make_async_remote_copy(
            src_ref=src,
            dst_ref=dst,
            send_sem=sem(base, 2 * index),
            recv_sem=sem(base, 2 * index + 1),
            device_id=target,
            device_id_type=MESH,
        )

    partners = [pair, across]
    if p.inside:
        partners += [(flipped(dp, bit), t) for bit in (1, 2, 4)]
    barrier = pltpu.get_barrier_semaphore()
    for partner in partners:
        pl.semaphore_signal(barrier, inc=1, device_id=partner, device_id_type=MESH)

    loads = [
        pltpu.make_async_copy(ins.retrieval.at[0], b.RET, sem(at.load, 0)),
        pltpu.make_async_copy(ins.att_in, b.ATI, sem(at.load, 1)),
        pltpu.make_async_copy(ins.att_out, b.ATO, sem(at.load, 2)),
    ]
    for copy in loads:
        copy.start()

    def load_ffn(f):
        return (
            pltpu.make_async_copy(ins.ffn_in.at[f], b.FFI, sem(at.load, 3)),
            pltpu.make_async_copy(ins.ffn_out.at[f], b.FFO, sem(at.load, 4)),
        )

    for copy in load_ffn(0):
        copy.start()

    pl.semaphore_wait(barrier, len(partners))

    def place(owner_x, owner_c, half):
        return pl.ds(pl.multiple_of((2 * owner_x + half) * CE + owner_c * HE, HE), HE)

    def enc_copy(half, target, index):
        src = ins.enc_input.at[pl.ds(half * HE, HE)]
        return remote(src, b.X.at[place(x, c, half)], at.ag, index, target)

    def enc_forward(half, index):
        rows = place(1 - x, c, half)
        return remote(b.X.at[rows], b.X.at[rows], at.ag, index, pair)

    dec_rows = pl.ds(pl.multiple_of(t * HD, HD), HD)
    far_rows = pl.ds(pl.multiple_of((t + 2 - 4 * x) * HD, HD), HD)

    def dec_copy(target, index):
        return remote(ins.dec_input, b.DX.at[dec_rows], at.ag, index, target)

    def dec_forward(index):
        return remote(b.DX.at[far_rows], b.DX.at[far_rows], at.ag, index, pair)

    ag_x = [enc_copy(0, across, 0), enc_copy(1, across, 1), dec_copy(across, 2)]
    ag_x.append(remote(ins.d_out, b.DOU.at[x], at.ag, 3, across))
    ag_p = [enc_copy(0, pair, 4), enc_copy(1, pair, 5), dec_copy(pair, 6)]
    ag_f = [enc_forward(0, 7), enc_forward(1, 8), dec_forward(9)]
    for copy in ag_x + ag_p:
        copy.start()
    own_copies = [
        pltpu.make_async_copy(
            ins.enc_input.at[pl.ds(0, HE)], b.X.at[place(x, c, 0)], sem(at.own, 0)
        ),
        pltpu.make_async_copy(
            ins.enc_input.at[pl.ds(HE, HE)], b.X.at[place(x, c, 1)], sem(at.own, 1)
        ),
        pltpu.make_async_copy(ins.dec_input, b.DX.at[dec_rows], sem(at.own, 2)),
        pltpu.make_async_copy(ins.d_out, b.DOU.at[x], sem(at.own, 3)),
    ]
    for copy in own_copies:
        copy.start()

    b.GAIN[...] = ins.ln_gain[...].astype(F32)
    b.SHIFT[...] = ins.ln_bias[...].astype(F32)
    b.AIB[...] = ins.att_in_bias[...].astype(F32)
    b.AOB[...] = ins.att_out_bias[...].astype(F32)
    b.FIB[...] = ins.ffn_in_bias[...].astype(F32)
    b.FOB[...] = ins.ffn_out_bias[...].astype(F32)
    b.SUM[...] = jnp.zeros((SUM_ROWS, D), F32)
    b.BIA[...] = jnp.zeros((4 * BIAS_ROWS, 256), F32)
    segments = ins.segment_ids[...].astype(F32)
    order = (0, 2, 1, 3, 4, 6, 5, 7)
    pieces = [segments[:, HE * o : HE * (o + 1)] for o in order]
    b.SEGR[...] = jnp.concatenate(pieces, axis=1)
    standing = jnp.concatenate(pieces, axis=0).T
    for k in range(8):
        b.SEGC[HE * k : HE * (k + 1), :] = standing[:, k : k + 1]

    lane_head = lax.broadcasted_iota(jnp.int32, (1, A), 1) // HEAD
    head_masks = [lane_head == h for h in range(heads)]
    zero16 = jnp.zeros((), BF16)

    def only_head(values, h):
        return jnp.where(head_masks[h], values, zero16)

    loads[0].wait()
    lanes = p.picks

    def count_block(index, carry):
        base = pl.multiple_of(index * 16, 16)
        for h in range(heads):
            halves = []
            for part in range(2):
                picks = b.RET[h, pl.ds(base + 8 * part, 8), :]
                high = lax.shift_right_logical(picks, 7)
                low = picks & 127
                swapped = (high & 4) | ((high & 1) << 1) | ((high >> 1) & 1)
                code = swapped * 8 + lax.broadcasted_iota(jnp.int32, (8, lanes), 0)
                codes = lax.broadcasted_iota(jnp.int32, (64, lanes), 0)
                lows = lax.broadcasted_iota(jnp.int32, (128, lanes), 0)
                left = jnp.concatenate(
                    [jnp.where(codes == code[k : k + 1, :], 1.0, 0.0).astype(BF16) for k in range(8)],
                    axis=1,
                )
                right = jnp.concatenate(
                    [jnp.where(lows == low[k : k + 1, :], 1.0, 0.0).astype(BF16) for k in range(8)],
                    axis=1,
                )
                halves.append(mm_nt(left, right))
            for k in range(8):
                value = jnp.concatenate([half[8 * k : 8 * k + 8] for half in halves], axis=0)
                b.CNT[pl.ds(h * S + base, 16), 128 * k : 128 * (k + 1)] = value.astype(BF16)
        return carry

    half_count = S // 32
    lax.fori_loop(0, half_count, count_block, 0)
    ag_x[0].wait_recv()
    ag_f[0].start()
    lax.fori_loop(half_count, 2 * half_count, count_block, 0)
    ag_x[1].wait_recv()
    ag_f[1].start()
    ag_x[2].wait_recv()
    ag_f[2].start()
    for copy in own_copies[:3]:
        copy.wait()
    for copy in ag_p:
        copy.wait_recv()
    loads[1].wait()
    loads[2].wait()
    for copy in ag_f:
        copy.wait_recv()

    def project(source, rows, index, target_q, target_k, target_v):
        if target_q is not None:
            bias = b.AIB[2 * index : 2 * index + 1, :]
            value = (mm_nt(source, b.ATI[3 * index]) + bias).astype(BF16)
            target_q[rows, :] = value * jnp.asarray(0.125, BF16)
        if target_k is not None:
            target_k[rows, :] = mm_nt(source, b.ATI[3 * index + 1]).astype(BF16)
            bias = b.AIB[2 * index + 1 : 2 * index + 2, :]
            target_v[rows, :] = (mm_nt(source, b.ATI[3 * index + 2]) + bias).astype(BF16)

    def enc_rows(i):
        return pl.ds(pl.multiple_of(i * CE, CE), CE)

    def dec_chunk(i):
        return pl.ds(pl.multiple_of(i * CD, CD), CD)

    def enc_mine(i):
        return pl.ds(pl.multiple_of(i * CE + c * HE, HE), HE)

    def dec_mine(i):
        return pl.ds(pl.multiple_of(i * CD + c * HD, HD), HD)

    def enc_sum(k):
        s = k % 2

        def pair_copy(i):
            return remote(b.PS.at[i], b.PR.at[i], at.enc, i, pair)

        def across_copy(i):
            return remote(b.XS.at[i], b.XR.at[s, i], at.enc, 4 + 4 * s + i, across)

        return (pair_copy, across_copy, b.OWN, b.PS, b.XS, b.PR, b.XR.at[s], HE)

    def dec_sum(k):
        s = k % 2

        def pair_copy(i):
            return remote(b.PSD.at[i], b.PRD.at[i], at.dec, i, pair)

        def across_copy(i):
            return remote(b.XSD.at[i], b.XRD.at[s, i], at.dec, 2 + 2 * s + i, across)

        return (
            pair_copy,
            across_copy,
            b.OWND,
            b.PSD,
            b.XSD,
            b.PRD,
            b.XRD.at[s],
            HD,
        )

    def pair_send(group, i, part):
        pair_copy, _, own, sent, _, _, _, half = group
        first, second = part[:half], part[half:]
        own[...] = jnp.where(c == 0, first, second)
        sent[i] = jnp.where(c == 0, second, first).astype(BF16)
        pair_copy(i).start()

    def pair_take(group, i):
        pair_copy, _, own, _, _, got, _, _ = group
        copy = pair_copy(i)
        copy.wait()
        return own[...] + got[i].astype(F32)

    def across_send(group, i):
        _, across_copy, _, _, sent, _, _, _ = group
        sent[i] = pair_take(group, i).astype(BF16)
        across_copy(i).start()

    def across_take(group, i):
        _, across_copy, _, _, sent, _, got, _ = group
        across_copy(i).wait()
        return sent[i].astype(F32) + got[i].astype(F32)

    def gather_copy(base, target, rows, i):
        return remote(target.at[rows], target.at[rows], base, i, pair)

    def gather_start(base, target, rows, i, value):
        target[rows, :] = value
        gather_copy(base, target, rows, i).start()

    def norm(index, value, xhat_ref, rstd_ref, i):
        center = value - jnp.mean(value, axis=-1, keepdims=True)
        rstd = lax.rsqrt(jnp.mean(center * center, axis=-1, keepdims=True) + EPS)
        xhat = center * rstd
        xhat_ref[i] = xhat
        rstd_ref[i] = rstd
        return xhat * b.GAIN[index : index + 1, :] + b.SHIFT[index : index + 1, :]

    def add_sum(row, value):
        b.SUM[row : row + 1, :] += column_sum(value)

    def norm_back(index, dy, xhat_ref, rstd_ref, i, bias_row):
        xhat = xhat_ref[i]
        scaled = dy * b.GAIN[index : index + 1, :]
        mean = jnp.mean(scaled, axis=-1, keepdims=True)
        along = jnp.mean(scaled * xhat, axis=-1, keepdims=True)
        dz = (scaled - mean - xhat * along) * rstd_ref[i]
        add_sum(ROW_GAIN + index, dy * xhat)
        add_sum(ROW_SHIFT + index, dy)
        add_sum(bias_row, dz)
        return dz

    def branch_of(total, bias, square):
        branch = total + bias
        add_sum(ROW_SQUARE + square, branch * branch)
        return branch

    def feed(rows, source, index, act_ref, slope_ref):
        for first in range(0, F, 256):
            cols = slice(first, first + 256)
            before = mm(source, b.FFI[:, cols]) + b.FIB[index : index + 1, cols]
            share = 0.5 + 0.5 * lax.erf(before * 0.7071067811865476)
            slope = share + before * jnp.exp(before * before * -0.5) * 0.3989422804014327
            act_ref[rows, cols] = (before * share).astype(BF16)
            slope_ref[rows, cols] = slope.astype(BF16)
        return mm_nt(act_ref[rows, :], b.FFO[...])

    def feed_back(rows, upstream, slope_ref):
        for first in range(0, F, 256):
            cols = slice(first, first + 256)
            dact = mm(upstream, b.FFO[:, cols])
            slope_ref[rows, cols] = (dact * slope_ref[rows, cols].astype(F32)).astype(BF16)
        return mm_nt(slope_ref[rows, :], b.FFI[...])

    block_rows = 128

    def project_enc(i, carry):
        rows = enc_rows(i)
        project(b.X[rows, :], rows, 0, b.Q, b.K, b.V)
        return carry

    lax.fori_loop(0, 4, project_enc, 0)

    def p_store(i):
        slot = i % 2 if isinstance(i, int) else lax.rem(i, jnp.int32(2))
        return pltpu.make_async_copy(b.BIG.at[2 * slot], outs.probs.at[i], sem(at.pst, slot))

    def p_load(i):
        slot = i % 2 if isinstance(i, int) else lax.rem(i, jnp.int32(2))
        return pltpu.make_async_copy(outs.probs.at[i], b.BIG.at[slot], sem(at.pst, slot))

    sum0 = enc_sum(0)

    def att_fwd(i, carry):
        rows = enc_rows(i)
        slot = lax.rem(i, jnp.int32(2))

        @pl.when(i >= 2)
        def _():
            p_store(i - 2).wait()

        def one_block(index, carry):
            shift = pl.multiple_of(index * block_rows, block_rows)
            own = pl.ds(pl.multiple_of(i * CE + shift, block_rows), block_rows)
            q = b.Q[own, :]
            same = b.SEGC[own, :] == b.SEGR[...]
            mixed = jnp.zeros((block_rows, A), F32)
            for h in range(heads):
                scores = mm_nt(only_head(q, h), b.K[...])
                scores = jnp.where(same, scores, NEG)
                expo = jnp.exp(scores - jnp.max(scores, axis=-1, keepdims=True))
                scale = 1.0 / jnp.sum(expo, axis=-1, keepdims=True)
                probs = (expo * scale).astype(BF16)
                b.BIG[2 * slot, pl.ds(pl.multiple_of(h * CE + shift, block_rows), block_rows), :] = probs
                mixed = jnp.where(head_masks[h], mm(probs, b.V[...]), mixed)
            b.O[own, :] = mixed.astype(BF16)
            return carry

        lax.fori_loop(0, CE // block_rows, one_block, 0)
        p_store(i).start()
        pair_send(sum0, i, mm(b.O[rows, :], b.ATO[0]))
        across_send(sum0, i)
        return carry

    lax.fori_loop(0, 4, att_fwd, 0)
    p_store(2).wait()
    p_store(3).wait()

    dsum0 = dec_sum(0)

    def dec_fwd(i, carry):
        rows = dec_chunk(i)
        q = b.QD[rows, :]
        row_index = lax.broadcasted_iota(jnp.int32, (CD, S), 0) + i * CD
        keep = row_index >= lax.broadcasted_iota(jnp.int32, (CD, S), 1)
        mixed = jnp.zeros((CD, A), F32)
        for h in range(heads):
            scores = jnp.where(keep, mm_nt(only_head(q, h), b.KD[...]), NEG)
            expo = jnp.exp(scores - jnp.max(scores, axis=-1, keepdims=True))
            scale = 1.0 / jnp.sum(expo, axis=-1, keepdims=True)
            probs = (expo * scale).astype(BF16)
            b.PD[pl.ds(pl.multiple_of(h * S + i * CD, CD), CD), :] = probs
            mixed = jnp.where(head_masks[h], mm(probs, b.VD[...]), mixed)
        joined = mixed.astype(BF16)
        b.OD[rows, :] = joined
        pair_send(dsum0, i, mm(joined, b.ATO[1]))
        across_send(dsum0, i)
        return carry

    whole = pl.ds(0, S)
    project(b.DX[...], whole, 1, b.QD, b.KD, b.VD)
    lax.fori_loop(0, 2, dec_fwd, 0)

    sum1 = enc_sum(1)
    for copy in load_ffn(0):
        copy.wait()

    def ffn_fwd(i, carry):
        mine = enc_mine(i)
        branch = branch_of(across_take(sum0, i), b.AOB[0:1, :], 0)
        hidden = norm(0, b.X[mine, :].astype(F32) + branch, b.XH0, b.RS0, i)
        b.RES[i] = hidden
        gather_start(at.H1, b.H1, mine, i, hidden.astype(BF16))
        gather_copy(at.H1, b.H1, mine, i).wait()
        rows = enc_rows(i)
        pair_send(sum1, i, feed(rows, b.H1[rows, :], 0, b.ACT0, b.GP0))
        across_send(sum1, i)
        return carry

    lax.fori_loop(0, 4, ffn_fwd, 0)
    for copy in load_ffn(1):
        copy.start()

    def dec_norm(i, carry):
        mine = dec_mine(i)
        branch = branch_of(across_take(dsum0, i), b.AOB[1:2, :], 2)
        hidden = norm(2, b.DX[mine, :].astype(F32) + branch, b.XH2, b.RS2, i)
        b.RESD[i] = hidden
        gather_start(at.G1, b.G1, mine, i, hidden.astype(BF16))
        return carry

    lax.fori_loop(0, 2, dec_norm, 0)
    for i in range(2):
        gather_copy(at.G1, b.G1, dec_mine(i), i).wait()
    project(b.G1[...], whole, 2, b.Q2, None, None)

    def memory_fwd(i, carry):
        mine = enc_mine(i)
        branch = branch_of(across_take(sum1, i), b.FOB[0:1, :], 1)
        hidden = norm(1, b.RES[i] + branch, b.XH1, b.RS1, i)
        add_sum(ROW_SQUARE + 5, hidden * hidden)
        gather_start(at.MEM, b.MEM, mine, i, hidden.astype(BF16))
        gather_copy(at.MEM, b.MEM, mine, i).wait()
        rows = enc_rows(i)
        project(b.MEM[rows, :], rows, 2, None, b.K2, b.V2)
        return carry

    lax.fori_loop(0, 4, memory_fwd, 0)

    dsum1 = dec_sum(1)

    def cross_fwd(i, carry):
        rows = dec_chunk(i)
        q = b.Q2[rows, :]
        mixed = jnp.zeros((CD, A), F32)
        for h in range(heads):
            own = pl.ds(pl.multiple_of(h * S + i * CD, CD), CD)
            weight = b.CNT[own, :].astype(F32)
            scores = jnp.where(weight > 0, mm_nt(only_head(q, h), b.K2[...]), NEG)
            expo = weight * jnp.exp(scores - jnp.max(scores, axis=-1, keepdims=True))
            scale = 1.0 / jnp.sum(expo, axis=-1, keepdims=True)
            probs = (expo * scale).astype(BF16)
            b.CNT[own, :] = probs
            mixed = jnp.where(head_masks[h], mm(probs, b.V2[...]), mixed)
        joined = mixed.astype(BF16)
        b.O2[rows, :] = joined
        pair_send(dsum1, i, mm(joined, b.ATO[2]))
        across_send(dsum1, i)
        return carry

    lax.fori_loop(0, 2, cross_fwd, 0)
    for copy in load_ffn(1):
        copy.wait()

    dsum2 = dec_sum(2)

    def dec_feed(i, carry):
        mine = dec_mine(i)
        branch = branch_of(across_take(dsum1, i), b.AOB[2:3, :], 3)
        hidden = norm(3, b.RESD[i] + branch, b.XH3, b.RS3, i)
        b.RESD[i] = hidden
        gather_start(at.G2, b.G2, mine, i, hidden.astype(BF16))
        gather_copy(at.G2, b.G2, mine, i).wait()
        rows = dec_chunk(i)
        pair_send(dsum2, i, feed(rows, b.G2[rows, :], 1, b.ACT1, b.GP1))
        across_send(dsum2, i)
        return carry

    lax.fori_loop(0, 2, dec_feed, 0)

    dsum3 = dec_sum(3)
    ag_x[3].wait_recv()
    own_copies[3].wait()

    def dec_turn(i, carry):
        mine = dec_mine(i)
        branch = branch_of(across_take(dsum2, i), b.FOB[1:2, :], 4)
        hidden = norm(4, b.RESD[i] + branch, b.XH4, b.RS4, i)
        add_sum(ROW_SQUARE + 6, hidden * hidden)
        b.G3S[i] = hidden.astype(BF16)
        dy = b.DOU[i].astype(F32)
        dz = norm_back(4, dy, b.XH4, b.RS4, i, ROW_FFN_OUT_BIAS + 1)
        b.RESD[i] = dz
        gather_start(at.E5, b.E5, mine, i, dz.astype(BF16))
        gather_copy(at.E5, b.E5, mine, i).wait()
        rows = dec_chunk(i)
        pair_send(dsum3, i, feed_back(rows, b.E5[rows, :], b.GP1))
        across_send(dsum3, i)
        return carry

    lax.fori_loop(0, 2, dec_turn, 0)
    outs.dec_output[...] = b.G3S[x]
    for copy in load_ffn(0):
        copy.start()

    def grad_place(k, j):
        if not p.inside:
            return j
        first, second, third = GRADS[k][2]
        return (j // first % 2) * 4 + (j // second % 2) * 2 + (j // third % 2)

    def transpose_into(source, rows):
        step = min(rows, 256)
        for first in range(0, rows, step):
            b.T[:, first : first + step] = source[first : first + step, :].T

    def grad_columns(k, rows, right, first, count):
        slot = k % SLOTS
        quarter = D // 2
        for a in range(2):
            value = mm(b.T[a * quarter : (a + 1) * quarter, :rows], right[...]).astype(BF16)
            for jj in range(4):
                where = grad_place(k, 4 * a + jj)
                b.GR[slot, where, :, first : first + count] = value[
                    jj * p.block : (jj + 1) * p.block, :
                ]

    def grad_copy(k, step):
        slot = k % SLOTS
        if not p.inside:
            return pltpu.make_async_copy(b.GR.at[slot], outs.grads.at[k], sem(at.grad, k))
        bits = GRADS[k][2]
        target = (flipped(dp, bits[step]), t)
        mine = [bit_of(dp, bit) for bit in bits]
        if step == 0:
            src = b.GR.at[slot, pl.ds(4 * (1 - mine[0]), 4)]
            return remote(src, b.R1.at[slot], at.grad, 3 * k, target)
        if step == 1:
            src = b.GR.at[slot, pl.ds(4 * mine[0] + 2 * (1 - mine[1]), 2)]
            return remote(src, b.R2.at[slot], at.grad, 3 * k + 1, target)
        src = b.GR.at[slot, pl.ds(4 * mine[0] + 2 * mine[1] + 1 - mine[2], 1)]
        return remote(src, b.R3.at[slot], at.grad, 3 * k + 2, target)

    def grad_step(k, step):
        if not p.inside:
            if step == 0:
                grad_copy(k, 0).start()
            if step == 3:
                grad_copy(k, 0).wait()
            return
        slot = k % SLOTS
        mine = [bit_of(dp, bit) for bit in GRADS[k][2]]
        if step > 0:
            grad_copy(k, step - 1).wait()
        if step == 1:
            for j in range(4):
                where = 4 * mine[0] + j
                total = b.GR[slot, where].astype(F32) + b.R1[slot, j].astype(F32)
                b.GR[slot, where] = total.astype(BF16)
        if step == 2:
            for j in range(2):
                where = 4 * mine[0] + 2 * mine[1] + j
                total = b.GR[slot, where].astype(F32) + b.R2[slot, j].astype(F32)
                b.GR[slot, where] = total.astype(BF16)
        if step == 3:
            where = 4 * mine[0] + 2 * mine[1] + mine[2]
            total = b.GR[slot, where].astype(F32) + b.R3[slot, 0].astype(F32)
            kind, index = GRADS[k][:2]
            if kind == ATT:
                for j in range(3):
                    outs.att_in[3 * index + j] = total[:, j * A : (j + 1) * A]
                outs.att_out[index] = total[:, 3 * A : 4 * A]
            elif kind == FFN_IN:
                outs.ffn_in[index] = total
            else:
                outs.ffn_out[index] = total
        if step > 0 and k + SLOTS < len(GRADS):
            later = (flipped(dp, GRADS[k + SLOTS][2][step - 1]), t)
            pl.semaphore_signal(
                free.at[3 * slot + step - 1], inc=1, device_id=later, device_id_type=MESH
            )
        if step < 3:
            if k >= SLOTS:
                pl.semaphore_wait(free.at[3 * slot + step], 1)
            grad_copy(k, step).start()

    def ffn_in_bias(f, dpre_ref):
        def gather_rows(i, total):
            block = dpre_ref[pl.ds(pl.multiple_of(i * CD, CD), CD), :]
            return total + column_sum(block.astype(F32))

        total = lax.fori_loop(0, dpre_ref.shape[0] // CD, gather_rows, jnp.zeros((1, F), F32))
        for owner in range(4):
            row = ROW_FFN_IN_BIAS + 4 * f + owner
            b.SUM[row : row + 1, :] = jnp.where(t == owner, total, 0.0)

    def att_bias(index, dq_ref, dv_ref):
        rows = []
        for ref in (dq_ref, dv_ref):
            rows.append(column_sum(ref[...].astype(F32)))
        for owner in range(4):
            for j in range(2):
                row = BIAS_ROWS * owner + 2 * index + j
                b.BIA[row : row + 1, :A] = jnp.where(t == owner, rows[j], 0.0)

    transpose_into(b.E5, S)
    grad_columns(0, S, b.ACT1, 0, F)
    grad_step(0, 0)
    transpose_into(b.G2, S)
    grad_columns(1, S, b.GP1, 0, F)
    grad_step(1, 0)
    ffn_in_bias(1, b.GP1)

    def dec_back(i, carry):
        mine = dec_mine(i)
        dy = b.RESD[i] + across_take(dsum3, i)
        dz = norm_back(3, dy, b.XH3, b.RS3, i, ROW_ATT_OUT_BIAS + 2)
        b.RESD[i] = dz
        gather_start(at.E4, b.E4, mine, i, dz.astype(BF16))
        return carry

    lax.fori_loop(0, 2, dec_back, 0)
    for i in range(2):
        gather_copy(at.E4, b.E4, dec_mine(i), i).wait()

    def attention_back(up_ref, q_ref, first, k_ref, v_ref, p_ref, d_ref, count, span):
        def one_block(index, carry):
            shift = pl.multiple_of(index * block_rows, block_rows)
            own = pl.ds(pl.multiple_of(first + shift, block_rows), block_rows)
            upstream, q = up_ref[own, :], q_ref[own, :]
            dq = jnp.zeros((block_rows, A), F32)
            for h in range(heads):
                rows = pl.ds(pl.multiple_of(h * count + shift, block_rows), block_rows)
                up = only_head(upstream, h)
                dprobs = mm_nt(up, v_ref[...])
                probs = p_ref[rows, :].astype(F32)
                inner = jnp.sum(probs * dprobs, axis=-1, keepdims=True)
                dscores = (probs * (dprobs - inner)).astype(BF16)
                b.DS[rows, :span] = dscores
                b.QS[rows, :] = only_head(q, h)
                b.DOS[rows, :] = up
                dq = jnp.where(head_masks[h], mm(dscores, k_ref[...]), dq)
            d_ref[own, :] = (dq * 0.125).astype(BF16)
            return carry

        lax.fori_loop(0, count // block_rows, one_block, 0)

    b.UPD[...] = mm_nt(b.E4[...], b.ATO[2]).astype(BF16)
    attention_back(b.UPD, b.Q2, 0, b.K2, b.V2, b.CNT, b.D2, S, R)
    sum2 = enc_sum(2)

    for i in range(4):
        cols = slice(i * CE, (i + 1) * CE)
        b.K2[cols, :] = mm_tn(b.DS[: heads * S, cols], b.QS[: heads * S, :]).astype(BF16)
        b.V2[cols, :] = mm_tn(b.CNT[:, cols], b.DOS[: heads * S, :]).astype(BF16)

    def memory_back(i, carry):
        rows = enc_rows(i)
        part = mm(b.K2[rows, :], b.ATI[7]) + mm(b.V2[rows, :], b.ATI[8])
        pair_send(sum2, i, part)
        across_send(sum2, i)
        return carry

    lax.fori_loop(0, 4, memory_back, 0)
    dsum4 = dec_sum(4)

    def query_back(i, carry):
        rows = dec_chunk(i)
        pair_send(dsum4, i, mm(b.D2[rows, :], b.ATI[6]))
        across_send(dsum4, i)
        return carry

    lax.fori_loop(0, 2, query_back, 0)

    grad_step(0, 1)
    grad_step(1, 1)
    transpose_into(b.G1, S)
    grad_columns(2, S, b.D2, 0, A)
    transpose_into(b.E4, S)
    grad_columns(2, S, b.O2, 3 * A, A)
    transpose_into(b.MEM, R)
    grad_columns(2, R, b.K2, A, A)
    grad_columns(2, R, b.V2, 2 * A, A)
    grad_step(2, 0)
    att_bias(2, b.D2, b.V2)

    sum3 = enc_sum(3)
    for copy in load_ffn(0):
        copy.wait()

    def ffn_back(i, carry):
        mine = enc_mine(i)
        dz = norm_back(1, across_take(sum2, i), b.XH1, b.RS1, i, ROW_FFN_OUT_BIAS)
        b.RES[i] = dz
        gather_start(at.E2, b.E2, mine, i, dz.astype(BF16))
        gather_copy(at.E2, b.E2, mine, i).wait()
        rows = enc_rows(i)
        pair_send(sum3, i, feed_back(rows, b.E2[rows, :], b.GP0))
        across_send(sum3, i)
        return carry

    lax.fori_loop(0, 4, ffn_back, 0)
    grad_step(0, 2)
    grad_step(1, 2)
    grad_step(2, 1)

    def dec_self(i, carry):
        mine = dec_mine(i)
        dy = b.RESD[i] + across_take(dsum4, i)
        dz = norm_back(2, dy, b.XH2, b.RS2, i, ROW_ATT_OUT_BIAS + 1)
        b.RESD[i] = dz
        gather_start(at.E3, b.E3, mine, i, dz.astype(BF16))
        return carry

    lax.fori_loop(0, 2, dec_self, 0)
    for i in range(2):
        gather_copy(at.E3, b.E3, dec_mine(i), i).wait()
    b.UPD[...] = mm_nt(b.E3[...], b.ATO[1]).astype(BF16)
    attention_back(b.UPD, b.QD, 0, b.KD, b.VD, b.PD, b.QD, S, S)
    b.KD[...] = mm_tn(b.DS[: heads * S, :S], b.QS[: heads * S, :]).astype(BF16)
    b.VD[...] = mm_tn(b.PD[...], b.DOS[: heads * S, :]).astype(BF16)

    dsum5 = dec_sum(5)
    for turn in range(2):
        i = 1 - x if turn == 0 else x
        rows = dec_chunk(i)
        part = (
            mm(b.QD[rows, :], b.ATI[3])
            + mm(b.KD[rows, :], b.ATI[4])
            + mm(b.VD[rows, :], b.ATI[5])
        )
        pair_send(dsum5, i, part)
        if turn == 0:
            across_send(dsum5, i)
        else:
            outs.dec_grad[...] = b.RESD[i] + pair_take(dsum5, i)

    grad_step(0, 3)
    transpose_into(b.DX, S)
    grad_columns(3, S, b.QD, 0, A)
    grad_columns(3, S, b.KD, A, A)
    grad_columns(3, S, b.VD, 2 * A, A)
    transpose_into(b.E3, S)
    grad_columns(3, S, b.OD, 3 * A, A)
    grad_step(3, 0)
    att_bias(1, b.QD, b.VD)
    grad_step(1, 3)
    grad_step(2, 2)
    transpose_into(b.E2, R)
    grad_columns(4, R, b.ACT0, 0, F)
    grad_step(4, 0)
    transpose_into(b.H1, R)
    grad_columns(5, R, b.GP0, 0, F)
    grad_step(5, 0)
    ffn_in_bias(0, b.GP0)
    grad_step(2, 3)
    grad_step(3, 1)

    p_load(0).start()
    p_load(1).start()
    b.DK[...] = jnp.zeros((R, A), F32)
    b.DV[...] = jnp.zeros((R, A), F32)

    def att_back(i, carry):
        mine = enc_mine(i)
        slot = lax.rem(i, jnp.int32(2))
        dy = b.RES[i] + across_take(sum3, i)
        dz = norm_back(0, dy, b.XH0, b.RS0, i, ROW_ATT_OUT_BIAS)
        b.RES[i] = dz
        gather_start(at.E1, b.MEM, mine, i, dz.astype(BF16))
        gather_copy(at.E1, b.MEM, mine, i).wait()
        rows = enc_rows(i)
        b.UP[rows, :] = mm_nt(b.MEM[rows, :], b.ATO[0]).astype(BF16)
        p_load(i).wait()
        p_ref = b.BIG.at[slot]
        attention_back(b.UP, b.Q, i * CE, b.K, b.V, p_ref, b.Q, CE, R)
        for j in range(4):
            cols = slice(j * CE, (j + 1) * CE)
            b.DK[cols, :] += mm_tn(b.DS[:, cols], b.QS[...])
            b.DV[cols, :] += mm_tn(b.BIG[slot, :, cols], b.DOS[...])

        @pl.when(i < 2)
        def _():
            p_load(i + 2).start()

        return carry

    lax.fori_loop(0, 4, att_back, 0)
    b.K[...] = b.DK[...].astype(BF16)
    b.V[...] = b.DV[...].astype(BF16)
    att_bias(0, b.Q, b.V)
    transpose_into(b.X, R)
    grad_columns(6, R, b.Q, 0, A)
    grad_columns(6, R, b.K, A, A)
    grad_columns(6, R, b.V, 2 * A, A)
    transpose_into(b.MEM, R)
    grad_columns(6, R, b.O, 3 * A, A)
    grad_step(6, 0)

    steps = [pair, across] + [(flipped(dp, bit), t) for bit in (1, 2, 4)]

    def sum_copy(step):
        return remote(b.SUM, b.SUMR.at[step], at.sum, step, steps[step])

    def bias_copy(step):
        return remote(b.BIA, b.BIAR.at[step], at.sum, 5 + step, steps[step])

    def sum_send(step):
        if p.inside:
            sum_copy(step).start()
            bias_copy(step).start()

    def sum_take(step):
        if p.inside:
            sum_copy(step).wait()
            b.SUM[...] += b.SUMR[step]
            bias_copy(step).wait()
            b.BIA[...] += b.BIAR[step]

    doubled = lax.broadcasted_iota(jnp.int32, (SUM_ROWS, 1), 0) < ROW_FFN_IN_BIAS
    b.SUM[...] = b.SUM[...] * jnp.where(doubled, 0.5, 1.0)
    sum_send(0)

    sum4 = enc_sum(4)
    for turn in range(4):
        i = 2 * (1 - x) + turn if turn < 2 else 2 * x + turn - 2
        rows = enc_rows(i)
        part = (
            mm(b.Q[rows, :], b.ATI[0])
            + mm(b.K[rows, :], b.ATI[1])
            + mm(b.V[rows, :], b.ATI[2])
        )
        pair_send(sum4, i, part)
        if turn < 2:
            across_send(sum4, i)
        else:
            own = (turn - 2) * HE
            outs.enc_grad[own : own + HE, :] = b.RES[i] + pair_take(sum4, i)
    sum_take(0)
    sum_send(1)
    grad_step(3, 2)
    grad_step(4, 1)
    grad_step(5, 1)
    grad_step(6, 1)
    sum_take(1)
    sum_send(2)
    grad_step(3, 3)
    grad_step(4, 2)
    grad_step(5, 2)
    grad_step(6, 2)
    sum_take(2)
    sum_send(3)

    _, dec_across, _, _, _, _, dec_got, _ = dsum5
    dec_across(1 - x).wait_send()
    dec_across(x).wait_recv()
    outs.dec_grad[...] += dec_got[x].astype(F32)
    _, enc_across, _, _, _, _, enc_got, _ = sum4
    for half in range(2):
        enc_across(2 * (1 - x) + half).wait_send()
        enc_across(2 * x + half).wait_recv()
        own = half * HE
        outs.enc_grad[own : own + HE, :] += enc_got[2 * x + half].astype(F32)
    sum_take(3)
    sum_send(4)
    grad_step(4, 3)
    grad_step(5, 3)
    grad_step(6, 3)
    sum_take(4)
    outs.sums[...] = b.SUM[...]
    outs.biases[...] = b.BIA[...]
    for copy in ag_x + ag_p + ag_f:
        copy.wait_send()


BIG_RESULTS = 7


def finish(p, counts, *refs):
    D, A, F = p.D, p.A, p.F
    n = BIG_RESULTS
    sources, (sums, biases) = refs[:n], refs[n : n + 2]
    targets, small, sems = refs[n + 2 : 2 * n + 2], refs[2 * n + 2 : -1], refs[-1]
    copies = [pltpu.make_async_copy(sources[k], targets[k], sems.at[k]) for k in range(n)]
    for copy in copies:
        copy.start()
    att_in_bias, att_out_bias, ffn_in_bias, ffn_out_bias, gain, shift, rms = small
    for owner in range(4):
        first = BIAS_ROWS * owner
        att_in_bias[:, owner * A : (owner + 1) * A] = biases[first : first + 6, :A]
        for f in range(2):
            row = ROW_FFN_IN_BIAS + 4 * f + owner
            ffn_in_bias[f : f + 1, owner * F : (owner + 1) * F] = sums[row : row + 1, :]
    att_out_bias[...] = sums[ROW_ATT_OUT_BIAS : ROW_ATT_OUT_BIAS + 3, :]
    ffn_out_bias[...] = sums[ROW_FFN_OUT_BIAS : ROW_FFN_OUT_BIAS + 2, :]
    gain[...] = sums[ROW_GAIN : ROW_GAIN + 5, :]
    shift[...] = sums[ROW_SHIFT : ROW_SHIFT + 5, :]
    values = jnp.zeros((1, 128), F32)
    lane = lax.broadcasted_iota(jnp.int32, (1, 128), 1)
    for k, count in enumerate(counts):
        row = sums[ROW_SQUARE + k : ROW_SQUARE + k + 1, :]
        values = jnp.where(lane == k, jnp.sum(row, axis=1, keepdims=True) * (1.0 / count), values)
    rms[...] = jnp.sqrt(values)[0, : len(counts)]
    for copy in copies:
        copy.wait()


def body(n_dp, *args):
    named = Inputs(*args)
    named = named._replace(
        att_in=jnp.transpose(named.att_in, (0, 2, 1)),
        att_out=jnp.transpose(named.att_out, (0, 2, 1)),
        retrieval=jnp.transpose(named.retrieval, (0, 2, 1, 3)),
    )
    p = Plan(named, n_dp)
    D, A, F = p.D, p.A, p.F
    shapes = Outputs(
        dec_output=((p.HD, D), BF16),
        enc_grad=((p.CE, D), F32),
        dec_grad=((p.HD, D), F32),
        sums=((SUM_ROWS, D), F32),
        biases=((4 * BIAS_ROWS, 256), F32),
        probs=((4, p.heads * p.CE, p.R), BF16),
    )
    if p.inside:
        shapes = shapes._replace(
            att_in=((9, p.block, A), F32),
            att_out=((3, p.block, A), F32),
            ffn_in=((2, p.block, F), F32),
            ffn_out=((2, p.block, F), F32),
        )
    else:
        shapes = shapes._replace(grads=((7, 8, p.block, D), BF16))
    hbm = pl.BlockSpec(memory_space=pl.ANY)
    vmem = pl.BlockSpec(memory_space=pltpu.VMEM)
    places, made_shapes, out_specs = [], [], []
    for position, value in enumerate(shapes):
        if value is None:
            places.append(None)
            continue
        places.append(len(made_shapes))
        made_shapes.append(jax.ShapeDtypeStruct(*value))
        out_specs.append(hbm if Outputs._fields[position] in (PROBS, ALL_GRADS) else vmem)
    results = pl.pallas_call(
        functools.partial(kernel, p, places),
        out_shape=made_shapes,
        in_specs=[hbm if fetched else vmem for fetched in IN_HBM],
        out_specs=out_specs,
        scratch_shapes=[
            *p.scratch.values(),
            pltpu.SemaphoreType.DMA((p.n_sems,)),
            pltpu.SemaphoreType.REGULAR((3 * SLOTS,)),
        ],
        compiler_params=pltpu.CompilerParams(
            collective_id=0, has_side_effects=True, vmem_limit_bytes=63 * 2**20
        ),
    )(*named)
    made = Outputs(*[None if place is None else results[place] for place in places])
    sums, biases = made.sums, made.biases
    if not p.inside:
        sums, biases = lax.psum((sums, biases), (DP, TENSOR))
        whole = made.grads.reshape(7, D, D).astype(F32)
        parts = lax.psum_scatter(whole, DP, scatter_dimension=1, tiled=True)
        found = {grad[:2]: parts[k] for k, grad in enumerate(GRADS)}
        att = [found[ATT, a] for a in range(3)]
        made = made._replace(
            att_in=jnp.stack([att[a][:, j * A : (j + 1) * A] for a in range(3) for j in range(3)]),
            att_out=jnp.stack([att[a][:, 3 * A : 4 * A] for a in range(3)]),
            ffn_in=jnp.stack([found[FFN_IN, f] for f in range(2)]),
            ffn_out=jnp.stack([found[FFN_OUT, f] for f in range(2)]),
        )
    devices = lax.axis_size(DP) * lax.axis_size(TENSOR)
    enc_count = 1.0 * p.CE * devices * D
    dec_count = 1.0 * p.HD * devices * D
    counts = (enc_count, enc_count, dec_count, dec_count, dec_count, enc_count, dec_count)
    large = (
        made.dec_output,
        made.enc_grad,
        made.dec_grad,
        made.att_in,
        made.att_out,
        made.ffn_in,
        made.ffn_out,
    )
    small = ((6, D), (3, D), (2, 4 * F), (2, D), (5, D), (5, D), (7,))
    done = pl.pallas_call(
        functools.partial(finish, p, counts),
        out_shape=[jax.ShapeDtypeStruct(value.shape, value.dtype) for value in large]
        + [jax.ShapeDtypeStruct(shape, F32) for shape in small],
        in_specs=[vmem] * (BIG_RESULTS + 2),
        out_specs=[hbm] * BIG_RESULTS + [vmem] * len(small),
        scratch_shapes=[pltpu.SemaphoreType.DMA((BIG_RESULTS,))],
    )(*large, sums, biases)
    dec_output, enc_grad, dec_grad, att_in, att_out, ffn_in, ffn_out = done[:BIG_RESULTS]
    att_in_bias, att_out_bias, ffn_in_bias, ffn_out_bias, gain, shift, rms = done[BIG_RESULTS:]
    return (
        dec_output,
        enc_grad,
        dec_grad,
        att_in,
        att_in_bias,
        att_out,
        att_out_bias,
        ffn_in,
        ffn_in_bias,
        ffn_out,
        ffn_out_bias,
        gain,
        shift,
        rms,
    )


def solution(mesh):
    rows = P((DP, TENSOR), None)
    placed = (
        rows,
        rows,
        P(DP, None),
        P(DP, None, TENSOR, None),
        P(None, None, TENSOR),
        P(None, TENSOR),
        P(None, None, TENSOR),
        P(),
        P(None, None, TENSOR),
        P(None, TENSOR),
        P(None, None, TENSOR),
        P(),
        P(),
        P(),
        rows,
    )
    split = P(None, DP, TENSOR)
    return jax.shard_map(
        functools.partial(body, mesh.shape[DP]),
        mesh=mesh,
        in_specs=placed,
        out_specs=(rows, rows, rows, split, P(), split, P(), split, P(), split, P(), P(), P(), P()),
        check_vma=False,
    )
```

```python
import functools
from types import SimpleNamespace
from typing import Any, NamedTuple

import jax
import jax.numpy as jnp
from jax import lax
from jax.experimental import pallas as pl
from jax.experimental.pallas import tpu as pltpu
from jax.sharding import PartitionSpec as P

HEAD = 64
EPS = 1e-05
NEG = -1e30
MESH = pl.DeviceIdType.MESH
DP, TENSOR = "dp", "tensor"
PROBS, ALL_GRADS = "probs", "grads"
F32 = jnp.float32
BF16 = jnp.bfloat16

ROW_ATT_OUT_BIAS = 0
ROW_FFN_OUT_BIAS = 3
ROW_GAIN = 5
ROW_SHIFT = 10
ROW_SQUARE = 15
ROW_FFN_IN_BIAS = 24
ROW_ATT_IN_BIAS = 30
SUM_ROWS = 40
LATE_ROWS = 8
LATE_NORM_ROWS = 3

ATT, FFN_IN, FFN_OUT = range(3)
GRADS = (
    (FFN_OUT, 1, (2, 1, 4), 0, 0, 2),
    (FFN_OUT, 1, (1, 4, 2), 0, 2, 4),
    (FFN_IN, 1, (1, 2, 4), 1, 0, 2),
    (FFN_IN, 1, (2, 1, 4), 1, 2, 4),
    (ATT, 2, (2, 1, 4), 2, 0, 2),
    (ATT, 2, (1, 2, 4), 2, 2, 4),
    (ATT, 1, (2, 1, 4), 4, 0, 2),
    (ATT, 1, (1, 2, 4), 4, 2, 4),
    (FFN_OUT, 0, (1, 2, 4), 3, 0, 2),
    (FFN_OUT, 0, (2, 1, 4), 3, 2, 4),
    (FFN_IN, 0, (2, 1, 4), 0, 0, 2),
    (FFN_IN, 0, (1, 4, 2), 0, 2, 4),
    (ATT, 0, (1, 4, 2), 1, 0, 2),
    (ATT, 0, (2, 1, 4), 1, 2, 4),
)
SLOTS = 5
WHOLE = tuple(grad[:2] for grad in GRADS if grad[4] == 0)


def next_in_slot(k):
    later = range(k + 1, len(GRADS))
    return [j for j in later if GRADS[j][3:] == GRADS[k][3:]]


def waits_for_slot(k):
    return any(k in next_in_slot(j) for j in range(k))


def mm(left, right):
    return jnp.dot(left, right, preferred_element_type=F32)


def mm_nt(left, right):
    return lax.dot_general(left, right, (((1,), (1,)), ((), ())), preferred_element_type=F32)


def mm_tn(left, right):
    return lax.dot_general(left, right, (((0,), (0,)), ((), ())), preferred_element_type=F32)


def bit_of(value, bit):
    return lax.rem(lax.div(value, jnp.int32(bit)), jnp.int32(2))


def flipped(value, bit):
    return value + bit - 2 * bit * bit_of(value, bit)


def column_sum(values):
    return jnp.sum(values, axis=0, keepdims=True)


class Inputs(NamedTuple):
    enc_input: Any
    dec_input: Any
    segment_ids: Any
    retrieval: Any
    att_in: Any
    att_in_bias: Any
    att_out: Any
    att_out_bias: Any
    ffn_in: Any
    ffn_in_bias: Any
    ffn_out: Any
    ffn_out_bias: Any
    ln_gain: Any
    ln_bias: Any
    d_out: Any


IN_HBM = Inputs(
    enc_input=True,
    dec_input=True,
    segment_ids=False,
    retrieval=True,
    att_in=True,
    att_in_bias=False,
    att_out=True,
    att_out_bias=False,
    ffn_in=True,
    ffn_in_bias=False,
    ffn_out=True,
    ffn_out_bias=False,
    ln_gain=False,
    ln_bias=False,
    d_out=True,
)


class Plan:
    def __init__(self, args, n_dp):
        self.D = D = args.enc_input.shape[1]
        self.CE = CE = args.enc_input.shape[0]
        self.HD = HD = args.dec_input.shape[0]
        self.HE = HE = CE // 2
        self.CD = 2 * HD
        self.R = R = 4 * CE
        self.S = S = 4 * HD
        self.A = A = args.att_in.shape[1]
        self.heads = heads = A // HEAD
        self.F = F = args.ffn_in.shape[2]
        self.picks = args.retrieval.shape[3]
        self.inside = n_dp == 8
        self.block = D // 8
        self.scratch = {}
        self.n_sems = 0
        self.at = SimpleNamespace()

        wide = ((R, D), BF16)
        short = ((S, D), BF16)
        enc_heads = ((R, A), BF16)
        dec_heads = ((S, A), BF16)
        enc_float = ((4, HE, D), F32)
        dec_float = ((2, HD, D), F32)
        enc_half = ((4, HE, D), BF16)
        dec_half = ((2, HD, D), BF16)
        enc_column = ((4, HE, 1), F32)
        dec_column = ((2, HD, 1), F32)
        stacked = ((heads * CE, A), BF16)
        self.vmem(
            ATI=((9, A, D), BF16),
            ATO=((3, A, D), BF16),
            FFI=((D, F), BF16),
            FFO=((D, F), BF16),
            RET=((heads, S, self.picks), jnp.int32),
        )
        self.vmem(X=wide, H1=wide, MEM=wide, E2=wide)
        self.vmem(DX=short, G1=short, G2=short, E5=short, E4=short)
        self.vmem(DOU=dec_half, G3S=dec_half)
        self.vmem(Q=enc_heads, K=enc_heads, V=enc_heads, O=enc_heads)
        self.vmem(K2=enc_heads, V2=enc_heads)
        turned = ((A, R), BF16)
        self.vmem(KT=turned, VT=turned, VT2=turned)
        self.vmem(KTD=((A, S), BF16), VTD=((A, S), BF16))
        self.vmem(QD=dec_heads, KD=dec_heads, VD=dec_heads, OD=dec_heads, UPD=dec_heads)
        self.vmem(Q2=dec_heads, O2=dec_heads, D2=dec_heads)
        self.vmem(DK=((A, R), F32), DV=((A, R), F32))
        self.vmem(BIG=((3, heads * CE, R), BF16), PD=((heads * S, S), BF16), QS=stacked, DOS=stacked)
        self.vmem(ACT0=((R, F), BF16), GP0=((R, F), BF16), ACT1=((S, F), BF16), GP1=((S, F), BF16))
        self.vmem(XH0=enc_float, XH1=enc_float, RES=enc_float)
        self.vmem(XH2=dec_float, XH3=dec_float, XH4=dec_float, RESD=dec_float)
        self.vmem(RS0=enc_column, RS1=enc_column, RS2=dec_column, RS3=dec_column, RS4=dec_column)
        self.vmem(SEGR=((1, R), F32), SEGC=((R, 1), F32), T=((D, R), BF16))
        self.vmem(OWN=((HE, D), F32), OWND=((HD, D), F32))
        self.vmem(PR=enc_half, PS=enc_half, XS=enc_half, XR=((2, 4, HE, D), BF16))
        self.vmem(PRD=dec_half, PSD=dec_half, XSD=dec_half, XRD=((2, 2, HD, D), BF16))
        self.vmem(GR=((SLOTS, 8, self.block, D), BF16))
        if self.inside:
            self.vmem(
                R1=((SLOTS, 4, self.block, D), BF16),
                R2=((SLOTS, 2, self.block, D), BF16),
                R3=((SLOTS, 1, self.block, D), BF16),
                SUMR=((5, SUM_ROWS, D), F32),
                LATR=((5, LATE_ROWS, D), F32),
            )
        self.vmem(SUM=((SUM_ROWS, D), F32), LATE=((LATE_ROWS, D), F32))
        self.vmem(GAIN=((5, D), F32), SHIFT=((5, D), F32))
        self.vmem(AIB=((6, A), F32), AOB=((3, D), F32), FIB=((2, F), F32), FOB=((2, D), F32))
        self.sem(load=8, own=4, ag=24, pst=2, enc=24, dec=12)
        self.sem(H1=8, MEM=8, E2=8, E1=8, G1=4, G2=4, E5=4, E4=4, E3=4)
        self.sem(grad=84, sum=30)

    def vmem(self, **buffers):
        for name, (shape, dtype) in buffers.items():
            self.scratch[name] = pltpu.VMEM(shape, dtype)

    def sem(self, **counts):
        for name, count in counts.items():
            setattr(self.at, name, self.n_sems)
            self.n_sems += count


class Outputs(NamedTuple):
    dec_output: Any
    enc_grad: Any
    dec_grad: Any
    sums: Any
    late: Any
    probs: Any
    grads: Any = None
    att_in: Any = None
    att_out: Any = None
    ffn_in: Any = None
    ffn_out: Any = None


def kernel(p, made, *refs):
    n_in = len(Inputs._fields)
    ins = Inputs(*refs[:n_in])
    outs = Outputs(*[None if index is None else refs[n_in + index] for index in made])
    n_out = sum(index is not None for index in made)
    b = SimpleNamespace(**dict(zip(p.scratch, refs[n_in + n_out : -2])))
    sems, free = refs[-2:]
    b.CNT, b.DS = b.BIG.at[1], b.BIG.at[2]
    b.KT2, b.UP, b.E3 = b.KT, b.K2, b.E5
    D, A, F, R, S, CE, HE, CD, HD = p.D, p.A, p.F, p.R, p.S, p.CE, p.HE, p.CD, p.HD
    heads, at = p.heads, p.at
    block_rows = 128

    t = lax.axis_index(TENSOR)
    dp = lax.axis_index(DP)
    x, c = lax.div(t, jnp.int32(2)), lax.rem(t, jnp.int32(2))
    pair = (dp, t + 1 - 2 * c)
    across = (dp, t + 2 - 4 * x)

    def sem(base, index):
        return sems.at[base + index]

    def remote(src, dst, base, index, target):
        return pltpu.make_async_remote_copy(
            src_ref=src,
            dst_ref=dst,
            send_sem=sem(base, 2 * index),
            recv_sem=sem(base, 2 * index + 1),
            device_id=target,
            device_id_type=MESH,
        )

    partners = [pair, across]
    if p.inside:
        partners += [(flipped(dp, bit), t) for bit in (1, 2, 4)]
    barrier = pltpu.get_barrier_semaphore()
    for partner in partners:
        pl.semaphore_signal(barrier, inc=1, device_id=partner, device_id_type=MESH)

    loads = [
        pltpu.make_async_copy(ins.retrieval.at[0], b.RET, sem(at.load, 0)),
        pltpu.make_async_copy(ins.att_in, b.ATI, sem(at.load, 1)),
        pltpu.make_async_copy(ins.att_out, b.ATO, sem(at.load, 2)),
    ]
    for copy in loads:
        copy.start()

    def load_ffn(f):
        return (
            pltpu.make_async_copy(ins.ffn_in.at[f], b.FFI, sem(at.load, 3)),
            pltpu.make_async_copy(ins.ffn_out.at[f], b.FFO, sem(at.load, 4)),
        )

    for copy in load_ffn(0):
        copy.start()

    pl.semaphore_wait(barrier, len(partners))

    def place(owner_x, owner_c, half):
        return pl.ds(pl.multiple_of((2 * owner_x + half) * CE + owner_c * HE, HE), HE)

    def enc_copy(half, target, index):
        src = ins.enc_input.at[pl.ds(half * HE, HE)]
        return remote(src, b.X.at[place(x, c, half)], at.ag, index, target)

    def enc_forward(half, index):
        rows = place(1 - x, c, half)
        return remote(b.X.at[rows], b.X.at[rows], at.ag, index, pair)

    dec_rows = pl.ds(pl.multiple_of(t * HD, HD), HD)
    far_rows = pl.ds(pl.multiple_of((t + 2 - 4 * x) * HD, HD), HD)

    def dec_copy(target, index):
        return remote(ins.dec_input, b.DX.at[dec_rows], at.ag, index, target)

    def dec_forward(index):
        return remote(b.DX.at[far_rows], b.DX.at[far_rows], at.ag, index, pair)

    ag_x = [enc_copy(0, across, 0), enc_copy(1, across, 1), dec_copy(across, 2)]
    ag_x.append(remote(ins.d_out, b.DOU.at[x], at.ag, 3, across))
    ag_p = [enc_copy(0, pair, 4), enc_copy(1, pair, 5), dec_copy(pair, 6)]
    ag_f = [enc_forward(0, 7), enc_forward(1, 8), dec_forward(9)]
    for copy in ag_x + ag_p:
        copy.start()
    own_copies = [
        pltpu.make_async_copy(
            ins.enc_input.at[pl.ds(0, HE)], b.X.at[place(x, c, 0)], sem(at.own, 0)
        ),
        pltpu.make_async_copy(
            ins.enc_input.at[pl.ds(HE, HE)], b.X.at[place(x, c, 1)], sem(at.own, 1)
        ),
        pltpu.make_async_copy(ins.dec_input, b.DX.at[dec_rows], sem(at.own, 2)),
        pltpu.make_async_copy(ins.d_out, b.DOU.at[x], sem(at.own, 3)),
    ]
    for copy in own_copies:
        copy.start()

    b.GAIN[...] = ins.ln_gain[...].astype(F32)
    b.SHIFT[...] = ins.ln_bias[...].astype(F32)
    b.AIB[...] = ins.att_in_bias[...].astype(F32)
    b.AOB[...] = ins.att_out_bias[...].astype(F32)
    b.FIB[...] = ins.ffn_in_bias[...].astype(F32)
    b.FOB[...] = ins.ffn_out_bias[...].astype(F32)
    b.SUM[...] = jnp.zeros((SUM_ROWS, D), F32)
    b.LATE[...] = jnp.zeros((LATE_ROWS, D), F32)
    segments = ins.segment_ids[...].astype(F32)
    order = (0, 2, 1, 3, 4, 6, 5, 7)
    pieces = [segments[:, HE * o : HE * (o + 1)] for o in order]
    b.SEGR[...] = jnp.concatenate(pieces, axis=1)
    standing = jnp.concatenate(pieces, axis=0).T
    for k in range(8):
        b.SEGC[HE * k : HE * (k + 1), :] = standing[:, k : k + 1]

    lane_head = lax.broadcasted_iota(jnp.int32, (1, A), 1) // HEAD
    head_masks = [lane_head == h for h in range(heads)]
    zero16 = jnp.zeros((), BF16)

    def only_head(values, h):
        return jnp.where(head_masks[h], values, zero16)

    loads[0].wait()
    lanes = p.picks

    def count_block(index, carry):
        base = pl.multiple_of(index * 16, 16)
        block = lax.div(index, jnp.int32(block_rows // 16))
        within = lax.rem(index, jnp.int32(block_rows // 16)) * 16
        first = pl.multiple_of(block * (heads * block_rows) + within, 16)
        for h in range(heads):
            halves = []
            for part in range(2):
                picks = b.RET[h, pl.ds(base + 8 * part, 8), :]
                high = lax.shift_right_logical(picks, 7)
                low = picks & 127
                swapped = (high & 4) | ((high & 1) << 1) | ((high >> 1) & 1)
                code = swapped * 8 + lax.broadcasted_iota(jnp.int32, (8, lanes), 0)
                codes = lax.broadcasted_iota(jnp.int32, (64, lanes), 0)
                lows = lax.broadcasted_iota(jnp.int32, (128, lanes), 0)
                left = jnp.concatenate(
                    [jnp.where(codes == code[k : k + 1, :], 1.0, 0.0).astype(BF16) for k in range(8)],
                    axis=1,
                )
                right = jnp.concatenate(
                    [jnp.where(lows == low[k : k + 1, :], 1.0, 0.0).astype(BF16) for k in range(8)],
                    axis=1,
                )
                halves.append(mm_nt(left, right))
            for k in range(8):
                value = jnp.concatenate([half[8 * k : 8 * k + 8] for half in halves], axis=0)
                b.CNT[pl.ds(first + h * block_rows, 16), 128 * k : 128 * (k + 1)] = value.astype(BF16)
        return carry

    def project(source, rows, index, target_q, target_k, target_v, turned_k, turned_v):
        if target_q is not None:
            bias = b.AIB[2 * index : 2 * index + 1, :]
            value = (mm_nt(source, b.ATI[3 * index]) + bias).astype(BF16)
            target_q[rows, :] = value * jnp.asarray(0.125, BF16)
        if target_k is not None:
            value = mm_nt(source, b.ATI[3 * index + 1]).astype(BF16)
            target_k[rows, :] = value
            turned_k[:, rows] = value.T
            bias = b.AIB[2 * index + 1 : 2 * index + 2, :]
            value = (mm_nt(source, b.ATI[3 * index + 2]) + bias).astype(BF16)
            target_v[rows, :] = value
            turned_v[:, rows] = value.T

    def enc_rows(i):
        return pl.ds(pl.multiple_of(i * CE, CE), CE)

    def dec_chunk(i):
        return pl.ds(pl.multiple_of(i * CD, CD), CD)

    def enc_mine(i):
        return pl.ds(pl.multiple_of(i * CE + c * HE, HE), HE)

    def dec_mine(i):
        return pl.ds(pl.multiple_of(i * CD + c * HD, HD), HD)

    def enc_sum(k):
        s = k % 2

        def pair_copy(i):
            return remote(b.PS.at[i], b.PR.at[i], at.enc, i, pair)

        def across_copy(i):
            return remote(b.XS.at[i], b.XR.at[s, i], at.enc, 4 + 4 * s + i, across)

        return (pair_copy, across_copy, b.OWN, b.PS, b.XS, b.PR, b.XR.at[s], HE)

    def dec_sum(k):
        s = k % 2

        def pair_copy(i):
            return remote(b.PSD.at[i], b.PRD.at[i], at.dec, i, pair)

        def across_copy(i):
            return remote(b.XSD.at[i], b.XRD.at[s, i], at.dec, 2 + 2 * s + i, across)

        return (
            pair_copy,
            across_copy,
            b.OWND,
            b.PSD,
            b.XSD,
            b.PRD,
            b.XRD.at[s],
            HD,
        )

    def pair_send(group, i, part):
        pair_copy, _, own, sent, _, _, _, half = group
        first, second = part[:half], part[half:]
        own[...] = jnp.where(c == 0, first, second)
        sent[i] = jnp.where(c == 0, second, first).astype(BF16)
        pair_copy(i).start()

    def pair_take(group, i):
        pair_copy, _, own, _, _, got, _, _ = group
        copy = pair_copy(i)
        copy.wait()
        return own[...] + got[i].astype(F32)

    def across_prepare(group, i):
        sent = group[4]
        sent[i] = pair_take(group, i).astype(BF16)

    def across_start(group, i):
        group[1](i).start()

    def across_send(group, i):
        across_prepare(group, i)
        across_start(group, i)

    def across_take(group, i):
        _, across_copy, _, _, sent, _, got, _ = group
        across_copy(i).wait()
        return sent[i].astype(F32) + got[i].astype(F32)

    def gather_copy(base, target, rows, i):
        return remote(target.at[rows], target.at[rows], base, i, pair)

    def gather_start(base, target, rows, i, value):
        target[rows, :] = value
        gather_copy(base, target, rows, i).start()

    def norm(index, value, xhat_ref, rstd_ref, i):
        center = value - jnp.mean(value, axis=-1, keepdims=True)
        rstd = lax.rsqrt(jnp.mean(center * center, axis=-1, keepdims=True) + EPS)
        xhat = center * rstd
        xhat_ref[i] = xhat
        rstd_ref[i] = rstd
        return xhat * b.GAIN[index : index + 1, :] + b.SHIFT[index : index + 1, :]

    def add_sum(row, value):
        b.SUM[row : row + 1, :] += column_sum(value)

    def norm_back(index, dy, xhat_ref, rstd_ref, i, bias_row):
        xhat = xhat_ref[i]
        scaled = dy * b.GAIN[index : index + 1, :]
        mean = jnp.mean(scaled, axis=-1, keepdims=True)
        along = jnp.mean(scaled * xhat, axis=-1, keepdims=True)
        dz = (scaled - mean - xhat * along) * rstd_ref[i]
        if index == 0:
            for row, value in enumerate((dz, dy * xhat, dy)):
                b.LATE[row : row + 1, :] += column_sum(value)
            return dz
        add_sum(ROW_GAIN + index, dy * xhat)
        add_sum(ROW_SHIFT + index, dy)
        add_sum(bias_row, dz)
        return dz

    def branch_of(total, bias, square):
        branch = total + bias
        add_sum(ROW_SQUARE + square, branch * branch)
        return branch

    def feed(rows, source, index, act_ref, slope_ref):
        for first in range(0, F, 256):
            cols = slice(first, first + 256)
            before = mm(source, b.FFI[:, cols]) + b.FIB[index : index + 1, cols]
            share = 0.5 + 0.5 * lax.erf(before * 0.7071067811865476)
            slope = share + before * jnp.exp(before * before * -0.5) * 0.3989422804014327
            act_ref[rows, cols] = (before * share).astype(BF16)
            slope_ref[rows, cols] = slope.astype(BF16)
        return mm_nt(act_ref[rows, :], b.FFO[...])

    def feed_back(rows, upstream, slope_ref):
        for first in range(0, F, 256):
            cols = slice(first, first + 256)
            dact = mm(upstream, b.FFO[:, cols])
            slope_ref[rows, cols] = (dact * slope_ref[rows, cols].astype(F32)).astype(BF16)
        return mm_nt(slope_ref[rows, :], b.FFI[...])

    def project_enc(i):
        rows = enc_rows(i)
        project(b.X[rows, :], rows, 0, b.Q, b.K, b.V, b.KT, b.VT)

    for copy in own_copies[:3]:
        copy.wait()
    loads[1].wait()
    loads[2].wait()
    ag_p[0].wait_recv()
    project_enc(2 * x)
    ag_p[1].wait_recv()
    project_enc(2 * x + 1)
    lax.fori_loop(0, 4, count_block, 0)
    ag_x[0].wait_recv()
    ag_f[0].start()
    lax.fori_loop(4, 8, count_block, 0)
    ag_x[1].wait_recv()
    ag_f[1].start()
    ag_f[0].wait_recv()
    project_enc(2 - 2 * x)
    ag_f[1].wait_recv()
    project_enc(3 - 2 * x)

    def p_store(i):
        slot = i % 2 if isinstance(i, int) else lax.rem(i, jnp.int32(2))
        return pltpu.make_async_copy(b.BIG.at[2 * slot], outs.probs.at[i], sem(at.pst, slot))

    def p_load(i):
        slot = i % 2 if isinstance(i, int) else lax.rem(i, jnp.int32(2))
        return pltpu.make_async_copy(outs.probs.at[i], b.BIG.at[slot], sem(at.pst, slot))

    stack = heads * block_rows

    def heads_stacked(values):
        return jnp.concatenate([only_head(values, h) for h in range(heads)], axis=0)

    def heads_joined(values):
        joined = values[:block_rows]
        for h in range(1, heads):
            own = values[h * block_rows : (h + 1) * block_rows]
            joined = jnp.where(head_masks[h], own, joined)
        return joined

    def attend(q, kt_ref, v_ref, p_ref, first, same):
        scores = mm(heads_stacked(q), kt_ref[...])
        for h in range(heads):
            rows = pl.ds(pl.multiple_of(first + h * block_rows, block_rows), block_rows)
            own = scores[h * block_rows : (h + 1) * block_rows]
            if same is None:
                weight = p_ref[rows, :].astype(F32)
                own = jnp.where(weight > 0, own, NEG)
                expo = weight * jnp.exp(own - jnp.max(own, axis=-1, keepdims=True))
            else:
                own = jnp.where(same, own, NEG)
                expo = jnp.exp(own - jnp.max(own, axis=-1, keepdims=True))
            scale = 1.0 / jnp.sum(expo, axis=-1, keepdims=True)
            p_ref[rows, :] = (expo * scale).astype(BF16)
        probs = p_ref[pl.ds(pl.multiple_of(first, block_rows), stack), :]
        return heads_joined(mm(probs, v_ref[...])).astype(BF16)

    sum0 = enc_sum(0)

    def att_fwd(i, carry):
        slot = lax.rem(i, jnp.int32(2))

        @pl.when(i >= 2)
        def _():
            p_store(i - 2).wait()

        @pl.when(i == 2)
        def _():
            ag_x[2].wait_recv()
            ag_f[2].start()

        def one_block(index, carry):
            own = pl.ds(pl.multiple_of(i * CE + index * block_rows, block_rows), block_rows)
            same = b.SEGC[own, :] == b.SEGR[...]
            p_ref = b.BIG.at[2 * slot]
            b.O[own, :] = attend(b.Q[own, :], b.KT, b.V, p_ref, index * stack, same)

            @pl.when((index == 0) & (i > 0))
            def _():
                across_send(sum0, i - 1)

            return carry

        lax.fori_loop(0, CE // block_rows, one_block, 0)
        p_store(i).start()
        pair_send(sum0, i, mm(b.O[enc_rows(i), :], b.ATO[0]))
        return carry

    lax.fori_loop(0, 4, att_fwd, 0)

    dsum0 = dec_sum(0)
    whole = pl.ds(0, S)
    ag_p[2].wait_recv()
    ag_f[2].wait_recv()
    project(b.DX[...], whole, 1, b.QD, b.KD, b.VD, b.KTD, b.VTD)
    across_send(sum0, 3)
    p_store(2).wait()
    p_store(3).wait()

    def dec_fwd(i, carry):
        rows = dec_chunk(i)
        row_index = lax.broadcasted_iota(jnp.int32, (CD, S), 0) + i * CD
        keep = row_index >= lax.broadcasted_iota(jnp.int32, (CD, S), 1)
        joined = attend(b.QD[rows, :], b.KTD, b.VD, b.PD, i * stack, keep)
        b.OD[rows, :] = joined
        pair_send(dsum0, i, mm(joined, b.ATO[1]))
        across_send(dsum0, i)
        return carry

    lax.fori_loop(0, 2, dec_fwd, 0)

    sum1 = enc_sum(1)
    for copy in load_ffn(0):
        copy.wait()

    def ffn_fwd(i, carry):
        mine = enc_mine(i)
        branch = branch_of(across_take(sum0, i), b.AOB[0:1, :], 0)
        hidden = norm(0, b.X[mine, :].astype(F32) + branch, b.XH0, b.RS0, i)
        b.RES[i] = hidden
        gather_start(at.H1, b.H1, mine, i, hidden.astype(BF16))
        count_block(8 + 2 * i, 0)
        gather_copy(at.H1, b.H1, mine, i).wait()
        rows = enc_rows(i)
        pair_send(sum1, i, feed(rows, b.H1[rows, :], 0, b.ACT0, b.GP0))
        count_block(9 + 2 * i, 0)
        across_send(sum1, i)
        return carry

    lax.fori_loop(0, 4, ffn_fwd, 0)
    for copy in load_ffn(1):
        copy.start()

    def dec_norm(i, carry):
        mine = dec_mine(i)
        branch = branch_of(across_take(dsum0, i), b.AOB[1:2, :], 2)
        hidden = norm(2, b.DX[mine, :].astype(F32) + branch, b.XH2, b.RS2, i)
        b.RESD[i] = hidden
        gather_start(at.G1, b.G1, mine, i, hidden.astype(BF16))
        return carry

    lax.fori_loop(0, 2, dec_norm, 0)
    for i in range(2):
        gather_copy(at.G1, b.G1, dec_mine(i), i).wait()
    project(b.G1[...], whole, 2, b.Q2, None, None, None, None)

    def memory_fwd(i, carry):
        mine = enc_mine(i)
        branch = branch_of(across_take(sum1, i), b.FOB[0:1, :], 1)
        hidden = norm(1, b.RES[i] + branch, b.XH1, b.RS1, i)
        add_sum(ROW_SQUARE + 5, hidden * hidden)
        gather_start(at.MEM, b.MEM, mine, i, hidden.astype(BF16))
        gather_copy(at.MEM, b.MEM, mine, i).wait()
        rows = enc_rows(i)
        project(b.MEM[rows, :], rows, 2, None, b.K2, b.V2, b.KT2, b.VT2)
        return carry

    lax.fori_loop(0, 4, memory_fwd, 0)

    dsum1 = dec_sum(1)

    def cross_fwd(i, carry):
        rows = dec_chunk(i)
        joined = attend(b.Q2[rows, :], b.KT2, b.V2, b.CNT, i * stack, None)
        b.O2[rows, :] = joined
        pair_send(dsum1, i, mm(joined, b.ATO[2]))
        across_send(dsum1, i)
        return carry

    lax.fori_loop(0, 2, cross_fwd, 0)
    for copy in load_ffn(1):
        copy.wait()

    dsum2 = dec_sum(2)

    def dec_feed(i, carry):
        mine = dec_mine(i)
        branch = branch_of(across_take(dsum1, i), b.AOB[2:3, :], 3)
        hidden = norm(3, b.RESD[i] + branch, b.XH3, b.RS3, i)
        b.RESD[i] = hidden
        gather_start(at.G2, b.G2, mine, i, hidden.astype(BF16))
        gather_copy(at.G2, b.G2, mine, i).wait()
        rows = dec_chunk(i)
        pair_send(dsum2, i, feed(rows, b.G2[rows, :], 1, b.ACT1, b.GP1))
        across_send(dsum2, i)
        return carry

    lax.fori_loop(0, 2, dec_feed, 0)

    dsum3 = dec_sum(3)
    ag_x[3].wait_recv()
    own_copies[3].wait()

    def dec_turn(i, carry):
        mine = dec_mine(i)
        branch = branch_of(across_take(dsum2, i), b.FOB[1:2, :], 4)
        hidden = norm(4, b.RESD[i] + branch, b.XH4, b.RS4, i)
        add_sum(ROW_SQUARE + 6, hidden * hidden)
        b.G3S[i] = hidden.astype(BF16)
        dy = b.DOU[i].astype(F32)
        dz = norm_back(4, dy, b.XH4, b.RS4, i, ROW_FFN_OUT_BIAS + 1)
        b.RESD[i] = dz
        gather_start(at.E5, b.E5, mine, i, dz.astype(BF16))
        gather_copy(at.E5, b.E5, mine, i).wait()
        rows = dec_chunk(i)
        pair_send(dsum3, i, feed_back(rows, b.E5[rows, :], b.GP1))
        across_send(dsum3, i)
        return carry

    lax.fori_loop(0, 2, dec_turn, 0)
    outs.dec_output[...] = b.G3S[x]
    for copy in load_ffn(0):
        copy.start()

    def grad_place(k, j):
        if not p.inside:
            return j
        first, second, third = GRADS[k][2]
        return (j // first % 2) * 4 + (j // second % 2) * 2 + (j // third % 2)

    def transpose_into(source, rows):
        step = min(rows, 256)
        for first in range(0, rows, step):
            b.T[:, first : first + step] = source[first : first + step, :].T

    def grad_columns(half, rows, right, first):
        slot = GRADS[half][3]
        quarter = D // 2
        count = right.shape[1]
        for a in range(2):
            value = mm(b.T[a * quarter : (a + 1) * quarter, :rows], right[...]).astype(BF16)
            for k in (half, half + 1):
                low, high = max(first, GRADS[k][4] * A), min(first + count, GRADS[k][5] * A)
                for jj in range(4 if low < high else 0):
                    where = grad_place(k, 4 * a + jj)
                    rows_own = slice(jj * p.block, (jj + 1) * p.block)
                    b.GR[slot, where, :, low:high] = value[rows_own, low - first : high - first]

    def both_steps(half, step):
        grad_step(half, step)
        grad_step(half + 1, step)

    def grad_copy(k, step):
        _, _, bits, slot, low, high = GRADS[k]
        cols = pl.ds(low * A, (high - low) * A)
        if not p.inside:
            whole_index = WHOLE.index(GRADS[k][:2])
            return pltpu.make_async_copy(b.GR.at[slot], outs.grads.at[whole_index], sem(at.grad, k))
        target = (flipped(dp, bits[step]), t)
        mine = [bit_of(dp, bit) for bit in bits]
        if step == 0:
            first, count, got = 4 * (1 - mine[0]), 4, b.R1
        elif step == 1:
            first, count, got = 4 * mine[0] + 2 * (1 - mine[1]), 2, b.R2
        else:
            first, count, got = 4 * mine[0] + 2 * mine[1] + 1 - mine[2], 1, b.R3
        src = b.GR.at[slot, pl.ds(first, count), :, cols]
        return remote(src, got.at[slot, :, :, cols], at.grad, 3 * k + step, target)

    def grad_step(k, step):
        kind, index, bits, slot, low, high = GRADS[k]
        if not p.inside:
            if high == 4 and step == 0:
                grad_copy(k, 0).start()
            if high == 4 and step == 3:
                grad_copy(k, 0).wait()
            return
        cols = slice(low * A, high * A)
        mine = [bit_of(dp, bit) for bit in bits]
        if step > 0:
            grad_copy(k, step - 1).wait()
        if step in (1, 2):
            got = b.R1 if step == 1 else b.R2
            base = 4 * mine[0] if step == 1 else 4 * mine[0] + 2 * mine[1]
            for j in range(got.shape[1]):
                total = b.GR[slot, base + j, :, cols].astype(F32) + got[slot, j, :, cols].astype(F32)
                b.GR[slot, base + j, :, cols] = total.astype(BF16)
        if step == 3:
            place_own = 4 * mine[0] + 2 * mine[1] + mine[2]
            total = b.GR[slot, place_own, :, cols].astype(F32) + b.R3[slot, 0, :, cols].astype(F32)
            if kind == ATT:
                for j in range(low, high):
                    part = total[:, (j - low) * A : (j - low + 1) * A]
                    if j < 3:
                        outs.att_in[3 * index + j] = part
                    else:
                        outs.att_out[index] = part
            elif kind == FFN_IN:
                outs.ffn_in[index, :, cols] = total
            else:
                outs.ffn_out[index, :, cols] = total
        if step > 0:
            for j in next_in_slot(k):
                later = (flipped(dp, GRADS[j][2][step - 1]), t)
                free_sem = free.at[3 * j + step - 1]
                pl.semaphore_signal(free_sem, inc=1, device_id=later, device_id_type=MESH)
        if step < 3:
            if waits_for_slot(k):
                pl.semaphore_wait(free.at[3 * k + step], 1)
            grad_copy(k, step).start()

    def ffn_in_bias(f, dpre_ref):
        def gather_rows(i, total):
            block = dpre_ref[pl.ds(pl.multiple_of(i * CD, CD), CD), :]
            return total + column_sum(block.astype(F32))

        total = lax.fori_loop(0, dpre_ref.shape[0] // CD, gather_rows, jnp.zeros((1, F), F32))
        for owner in range(4):
            row = ROW_FFN_IN_BIAS + 4 * f + owner
            b.SUM[row : row + 1, :] = jnp.where(t == owner, total, 0.0)

    def att_bias(index, dq_ref, dv_ref):
        rows = []
        for ref in (dq_ref, dv_ref):
            rows.append(column_sum(ref[...].astype(F32)))
        table, first = (b.LATE, LATE_NORM_ROWS) if index == 0 else (b.SUM, ROW_ATT_IN_BIAS + 2 * index)
        for owner in range(4):
            for j in range(2):
                cols = slice(owner * A, (owner + 1) * A)
                table[first + j : first + j + 1, cols] = jnp.where(t == owner, rows[j], 0.0)

    transpose_into(b.E5, S)
    grad_columns(0, S, b.ACT1, 0)
    both_steps(0, 0)
    transpose_into(b.G2, S)
    grad_columns(2, S, b.GP1, 0)
    both_steps(2, 0)
    ffn_in_bias(1, b.GP1)

    def dec_back(i, carry):
        mine = dec_mine(i)
        dy = b.RESD[i] + across_take(dsum3, i)
        dz = norm_back(3, dy, b.XH3, b.RS3, i, ROW_ATT_OUT_BIAS + 2)
        b.RESD[i] = dz
        gather_start(at.E4, b.E4, mine, i, dz.astype(BF16))
        return carry

    lax.fori_loop(0, 2, dec_back, 0)
    for i in range(2):
        gather_copy(at.E4, b.E4, dec_mine(i), i).wait()

    def attention_back(up_ref, q_ref, o_ref, first, k_ref, vt_ref, p_ref, d_ref, count, span):
        def one_block(index):
            own = pl.ds(pl.multiple_of(first + index * block_rows, block_rows), block_rows)
            stacked = slice(index * stack, (index + 1) * stack)
            upstream = up_ref[own, :]
            along = upstream.astype(F32) * o_ref[own, :].astype(F32)
            ups = heads_stacked(upstream)
            b.DOS[stacked, :] = ups
            b.QS[stacked, :] = heads_stacked(q_ref[own, :])
            dprobs = mm(ups, vt_ref[...])
            for h in range(heads):
                rows = slice(index * stack + h * block_rows, index * stack + (h + 1) * block_rows)
                inner = jnp.sum(jnp.where(head_masks[h], along, 0.0), axis=-1, keepdims=True)
                part = dprobs[h * block_rows : (h + 1) * block_rows] - inner
                b.DS[rows, :span] = (p_ref[rows, :].astype(F32) * part).astype(BF16)
            dq = heads_joined(mm(b.DS[stacked, :span], k_ref[...]))
            d_ref[own, :] = (dq * 0.125).astype(BF16)

        for index in range(count // block_rows):
            one_block(index)

    b.UPD[...] = mm_nt(b.E4[...], b.ATO[2]).astype(BF16)
    attention_back(b.UPD, b.Q2, b.O2, jnp.int32(0), b.K2, b.VT2, b.CNT, b.D2, S, R)
    sum2 = enc_sum(2)

    for i in range(4):
        cols = slice(i * CE, (i + 1) * CE)
        b.K2[cols, :] = mm_tn(b.QS[: heads * S, :], b.DS[: heads * S, cols]).astype(BF16).T
        b.V2[cols, :] = mm_tn(b.DOS[: heads * S, :], b.CNT[:, cols]).astype(BF16).T

    def memory_back(i):
        rows = slice(i * CE, (i + 1) * CE)
        return mm(b.K2[rows, :], b.ATI[7]) + mm(b.V2[rows, :], b.ATI[8])

    def query_back(i):
        return mm(b.D2[i * CD : (i + 1) * CD, :], b.ATI[6])

    dsum4 = dec_sum(4)
    pair_send(sum2, 0, memory_back(0))
    part = memory_back(1)
    across_send(sum2, 0)
    pair_send(sum2, 1, part)
    transpose_into(b.G1, S)
    grad_columns(4, S, b.D2, 0)
    across_send(sum2, 1)
    transpose_into(b.MEM, R)
    grad_columns(4, R, b.K2, A)
    grad_step(4, 0)
    grad_columns(4, R, b.V2, 2 * A)
    transpose_into(b.E4, S)
    grad_columns(4, S, b.O2, 3 * A)
    grad_step(5, 0)
    grad_step(1, 1)
    sends = [(dsum4, i, query_back) for i in (0, 1)]
    sends += [(sum2, i, memory_back) for i in (2, 3)]
    before = None
    for group, i, part_of in sends:
        if group is sum2 and i == 2:
            grad_step(0, 1)
        part = part_of(i)
        if before is not None:
            across_send(*before)
        pair_send(group, i, part)
        before = (group, i)
    att_bias(2, b.D2, b.V2)
    across_send(*before)

    sum3 = enc_sum(3)
    for copy in load_ffn(0):
        copy.wait()

    def ffn_back(i, carry):
        mine = enc_mine(i)

        @pl.when(i == 1)
        def _():
            grad_step(5, 1)

        dy = across_take(sum2, i)

        @pl.when(i == 0)
        def _():
            grad_step(2, 1)

        @pl.when(i >= 2)
        def _():
            across_start(sum3, i - 2)

        dz = norm_back(1, dy, b.XH1, b.RS1, i, ROW_FFN_OUT_BIAS)
        b.RES[i] = dz
        gather_start(at.E2, b.E2, mine, i, dz.astype(BF16))

        @pl.when(i >= 1)
        def _():
            across_prepare(sum3, i - 1)

        gather_copy(at.E2, b.E2, mine, i).wait()
        rows = enc_rows(i)
        pair_send(sum3, i, feed_back(rows, b.E2[rows, :], b.GP0))
        return carry

    lax.fori_loop(0, 2, ffn_back, 0)
    grad_step(1, 2)
    grad_step(3, 1)
    grad_step(0, 2)

    def dec_self(i, carry):
        mine = dec_mine(i)
        dy = b.RESD[i] + across_take(dsum4, i)
        dz = norm_back(2, dy, b.XH2, b.RS2, i, ROW_ATT_OUT_BIAS + 1)
        b.RESD[i] = dz
        gather_start(at.E3, b.E3, mine, i, dz.astype(BF16))
        return carry

    lax.fori_loop(0, 2, dec_self, 0)
    for i in range(2):
        gather_copy(at.E3, b.E3, dec_mine(i), i).wait()
    b.UPD[...] = mm_nt(b.E3[...], b.ATO[1]).astype(BF16)
    attention_back(b.UPD, b.QD, b.OD, jnp.int32(0), b.KD, b.VTD, b.PD, b.QD, S, S)
    b.KD[...] = mm_tn(b.DS[: heads * S, :S], b.QS[: heads * S, :]).astype(BF16)
    b.VD[...] = mm_tn(b.PD[...], b.DOS[: heads * S, :]).astype(BF16)

    dsum5 = dec_sum(5)
    for turn in range(2):
        i = 1 - x if turn == 0 else x
        rows = dec_chunk(i)
        part = (
            mm(b.QD[rows, :], b.ATI[3])
            + mm(b.KD[rows, :], b.ATI[4])
            + mm(b.VD[rows, :], b.ATI[5])
        )
        pair_send(dsum5, i, part)
        if turn == 0:
            across_send(dsum5, i)
        else:
            outs.dec_grad[...] = b.RESD[i] + pair_take(dsum5, i)

    transpose_into(b.DX, S)
    grad_columns(6, S, b.QD, 0)
    grad_columns(6, S, b.KD, A)
    grad_step(4, 1)
    grad_step(6, 0)
    grad_columns(6, S, b.VD, 2 * A)
    transpose_into(b.E3, S)
    grad_columns(6, S, b.OD, 3 * A)
    grad_step(2, 2)
    grad_step(7, 0)
    att_bias(1, b.QD, b.VD)
    lax.fori_loop(2, 4, ffn_back, 0)
    across_start(sum3, 2)
    across_send(sum3, 3)
    grad_step(1, 3)

    steps = [pair, across] + [(flipped(dp, bit), t) for bit in (1, 2, 4)]

    def total_copy(buffer, got, first, step):
        return remote(buffer, got.at[step], at.sum, first + step, steps[step])

    def total_step(buffer, got, first, step):
        if not p.inside:
            return
        if step > 0:
            total_copy(buffer, got, first, step - 1).wait()
            buffer[...] += got[step - 1]
        if step < len(steps):
            total_copy(buffer, got, first, step).start()

    def early_step(step):
        total_step(b.SUM, b.SUMR if p.inside else None, 0, step)

    def late_step(step):
        total_step(b.LATE, b.LATR if p.inside else None, 5, step)

    doubled = lax.broadcasted_iota(jnp.int32, (SUM_ROWS, 1), 0) < ROW_FFN_IN_BIAS
    ffn_in_bias(0, b.GP0)
    b.SUM[...] = b.SUM[...] * jnp.where(doubled, 0.5, 1.0)
    transpose_into(b.E2, R)
    grad_columns(8, R, b.ACT0, 0)
    both_steps(8, 0)
    grad_step(6, 1)
    grad_step(0, 3)
    transpose_into(b.H1, R)
    grad_columns(10, R, b.GP0, 0)
    grad_step(3, 2)
    early_step(0)
    both_steps(10, 0)
    grad_step(2, 3)
    grad_step(4, 2)

    p_load(0).start()
    p_load(1).start()
    b.DK[...] = jnp.zeros((A, R), F32)
    b.DV[...] = jnp.zeros((A, R), F32)

    def att_back(i, carry):
        mine = enc_mine(i)
        slot = lax.rem(i, jnp.int32(2))
        dy = b.RES[i] + across_take(sum3, i)
        dz = norm_back(0, dy, b.XH0, b.RS0, i, ROW_ATT_OUT_BIAS)
        b.RES[i] = dz
        gather_start(at.E1, b.MEM, mine, i, dz.astype(BF16))

        @pl.when(i == 0)
        def _():
            grad_step(7, 1)
            early_step(1)
            grad_step(5, 2)

        @pl.when(i == 2)
        def _():
            grad_step(6, 2)

        @pl.when(i == 3)
        def _():
            grad_step(11, 1)
            grad_step(9, 1)

        gather_copy(at.E1, b.MEM, mine, i).wait()
        rows = enc_rows(i)
        b.UP[rows, :] = mm_nt(b.MEM[rows, :], b.ATO[0]).astype(BF16)
        p_load(i).wait()
        p_ref = b.BIG.at[slot]
        attention_back(b.UP, b.Q, b.O, i * CE, b.K, b.VT, p_ref, b.Q, CE, R)
        for j in range(2):
            cols = slice(2 * j * CE, 2 * (j + 1) * CE)
            b.DK[:, cols] += mm_tn(b.QS[...], b.DS[:, cols])
            b.DV[:, cols] += mm_tn(b.DOS[...], b.BIG[slot, :, cols])

        @pl.when(i < 2)
        def _():
            p_load(i + 2).start()

        return carry

    lax.fori_loop(0, 4, att_back, 0)
    for j in range(4):
        cols = slice(j * CE, (j + 1) * CE)
        b.K[cols, :] = b.DK[:, cols].astype(BF16).T
        b.V[cols, :] = b.DV[:, cols].astype(BF16).T
    grad_step(8, 1)
    grad_step(3, 3)
    att_bias(0, b.Q, b.V)
    norm_rows = lax.broadcasted_iota(jnp.int32, (LATE_ROWS, 1), 0) < LATE_NORM_ROWS
    b.LATE[...] = b.LATE[...] * jnp.where(norm_rows, 0.5, 1.0)
    late_step(0)
    grad_step(5, 3)
    grad_step(6, 3)
    early_step(2)
    transpose_into(b.X, R)
    grad_columns(12, R, b.Q, 0)
    grad_columns(12, R, b.K, A)
    grad_step(12, 0)
    late_step(1)
    grad_columns(12, R, b.V, 2 * A)
    transpose_into(b.MEM, R)
    grad_columns(12, R, b.O, 3 * A)
    grad_step(13, 0)
    grad_step(7, 2)
    grad_step(10, 1)

    sum4 = enc_sum(4)
    for turn in range(4):
        i = 2 * (1 - x) + turn if turn < 2 else 2 * x + turn - 2
        rows = enc_rows(i)
        part = (
            mm(b.Q[rows, :], b.ATI[0])
            + mm(b.K[rows, :], b.ATI[1])
            + mm(b.V[rows, :], b.ATI[2])
        )
        pair_send(sum4, i, part)
        if turn == 0:
            grad_step(9, 2)
            late_step(2)
            across_send(sum4, i)
        elif turn == 1:
            across_send(sum4, i)
            grad_step(8, 2)
            grad_step(10, 2)
            grad_step(7, 3)
        else:
            own = (turn - 2) * HE
            outs.enc_grad[own : own + HE, :] = b.RES[i] + pair_take(sum4, i)
    late_step(3)
    early_step(3)
    grad_step(8, 3)
    grad_step(12, 1)
    grad_step(13, 1)
    grad_step(9, 3)
    late_step(4)
    grad_step(13, 2)
    grad_step(11, 2)
    late_step(5)

    _, dec_across, _, _, _, _, dec_got, _ = dsum5
    dec_across(1 - x).wait_send()
    dec_across(x).wait_recv()
    outs.dec_grad[...] += dec_got[x].astype(F32)
    outs.late[...] = b.LATE[...]
    early_step(4)
    grad_step(12, 2)
    grad_step(10, 3)
    grad_step(13, 3)
    _, enc_across, _, _, _, _, enc_got, _ = sum4
    for half in range(2):
        enc_across(2 * (1 - x) + half).wait_send()
        enc_across(2 * x + half).wait_recv()
        own = half * HE
        outs.enc_grad[own : own + HE, :] += enc_got[2 * x + half].astype(F32)
    grad_step(4, 3)
    grad_step(12, 3)
    grad_step(11, 3)
    early_step(5)
    outs.sums[...] = b.SUM[...]
    for copy in ag_x + ag_p + ag_f:
        copy.wait_send()


BIG_RESULTS = 7


def finish(p, counts, *refs):
    D, A, F = p.D, p.A, p.F
    n = BIG_RESULTS
    sources, (sums, late) = refs[:n], refs[n : n + 2]
    targets, small, sems = refs[n + 2 : 2 * n + 2], refs[2 * n + 2 : -1], refs[-1]
    copies = [pltpu.make_async_copy(sources[k], targets[k], sems.at[k]) for k in range(n)]
    for copy in copies:
        copy.start()
    att_in_bias, att_out_bias, ffn_in_bias, ffn_out_bias, gain, shift, rms = small
    att_in_bias[:2, :] = late[LATE_NORM_ROWS : LATE_NORM_ROWS + 2, :]
    att_in_bias[2:, :] = sums[ROW_ATT_IN_BIAS + 2 : ROW_ATT_IN_BIAS + 6, :]
    for owner in range(4):
        for f in range(2):
            row = ROW_FFN_IN_BIAS + 4 * f + owner
            ffn_in_bias[f : f + 1, owner * F : (owner + 1) * F] = sums[row : row + 1, :]
    att_out_bias[...] = sums[ROW_ATT_OUT_BIAS : ROW_ATT_OUT_BIAS + 3, :]
    ffn_out_bias[...] = sums[ROW_FFN_OUT_BIAS : ROW_FFN_OUT_BIAS + 2, :]
    gain[...] = sums[ROW_GAIN : ROW_GAIN + 5, :]
    shift[...] = sums[ROW_SHIFT : ROW_SHIFT + 5, :]
    for row, target in enumerate((att_out_bias, gain, shift)):
        target[0:1, :] = late[row : row + 1, :]
    values = jnp.zeros((1, 128), F32)
    lane = lax.broadcasted_iota(jnp.int32, (1, 128), 1)
    for k, count in enumerate(counts):
        row = sums[ROW_SQUARE + k : ROW_SQUARE + k + 1, :]
        values = jnp.where(lane == k, jnp.sum(row, axis=1, keepdims=True) * (1.0 / count), values)
    rms[...] = jnp.sqrt(values)[0, : len(counts)]
    for copy in copies:
        copy.wait()


def body(n_dp, *args):
    named = Inputs(*args)
    named = named._replace(
        att_in=jnp.transpose(named.att_in, (0, 2, 1)),
        att_out=jnp.transpose(named.att_out, (0, 2, 1)),
        retrieval=jnp.transpose(named.retrieval, (0, 2, 1, 3)),
    )
    p = Plan(named, n_dp)
    D, A, F = p.D, p.A, p.F
    shapes = Outputs(
        dec_output=((p.HD, D), BF16),
        enc_grad=((p.CE, D), F32),
        dec_grad=((p.HD, D), F32),
        sums=((SUM_ROWS, D), F32),
        late=((LATE_ROWS, D), F32),
        probs=((4, p.heads * p.CE, p.R), BF16),
    )
    if p.inside:
        shapes = shapes._replace(
            att_in=((9, p.block, A), F32),
            att_out=((3, p.block, A), F32),
            ffn_in=((2, p.block, F), F32),
            ffn_out=((2, p.block, F), F32),
        )
    else:
        shapes = shapes._replace(grads=((7, 8, p.block, D), BF16))
    hbm = pl.BlockSpec(memory_space=pl.ANY)
    vmem = pl.BlockSpec(memory_space=pltpu.VMEM)
    places, made_shapes, out_specs = [], [], []
    for position, value in enumerate(shapes):
        if value is None:
            places.append(None)
            continue
        places.append(len(made_shapes))
        made_shapes.append(jax.ShapeDtypeStruct(*value))
        out_specs.append(hbm if Outputs._fields[position] in (PROBS, ALL_GRADS) else vmem)
    results = pl.pallas_call(
        functools.partial(kernel, p, places),
        out_shape=made_shapes,
        in_specs=[hbm if fetched else vmem for fetched in IN_HBM],
        out_specs=out_specs,
        scratch_shapes=[
            *p.scratch.values(),
            pltpu.SemaphoreType.DMA((p.n_sems,)),
            pltpu.SemaphoreType.REGULAR((3 * len(GRADS),)),
        ],
        compiler_params=pltpu.CompilerParams(
            collective_id=0, has_side_effects=True, vmem_limit_bytes=63 * 2**20
        ),
    )(*named)
    made = Outputs(*[None if place is None else results[place] for place in places])
    sums, late = made.sums, made.late
    if not p.inside:
        sums, late = lax.psum((sums, late), (DP, TENSOR))
        whole = made.grads.reshape(7, D, D).astype(F32)
        parts = lax.psum_scatter(whole, DP, scatter_dimension=1, tiled=True)
        found = {grad: parts[k] for k, grad in enumerate(WHOLE)}
        att = [found[ATT, a] for a in range(3)]
        made = made._replace(
            att_in=jnp.stack([att[a][:, j * A : (j + 1) * A] for a in range(3) for j in range(3)]),
            att_out=jnp.stack([att[a][:, 3 * A : 4 * A] for a in range(3)]),
            ffn_in=jnp.stack([found[FFN_IN, f] for f in range(2)]),
            ffn_out=jnp.stack([found[FFN_OUT, f] for f in range(2)]),
        )
    devices = lax.axis_size(DP) * lax.axis_size(TENSOR)
    enc_count = 1.0 * p.CE * devices * D
    dec_count = 1.0 * p.HD * devices * D
    counts = (enc_count, enc_count, dec_count, dec_count, dec_count, enc_count, dec_count)
    large = (
        made.dec_output,
        made.enc_grad,
        made.dec_grad,
        made.att_in,
        made.att_out,
        made.ffn_in,
        made.ffn_out,
    )
    small = ((6, D), (3, D), (2, 4 * F), (2, D), (5, D), (5, D), (7,))
    done = pl.pallas_call(
        functools.partial(finish, p, counts),
        out_shape=[jax.ShapeDtypeStruct(value.shape, value.dtype) for value in large]
        + [jax.ShapeDtypeStruct(shape, F32) for shape in small],
        in_specs=[vmem] * (BIG_RESULTS + 2),
        out_specs=[hbm] * BIG_RESULTS + [vmem] * len(small),
        scratch_shapes=[pltpu.SemaphoreType.DMA((BIG_RESULTS,))],
    )(*large, sums, late)
    dec_output, enc_grad, dec_grad, att_in, att_out, ffn_in, ffn_out = done[:BIG_RESULTS]
    att_in_bias, att_out_bias, ffn_in_bias, ffn_out_bias, gain, shift, rms = done[BIG_RESULTS:]
    return (
        dec_output,
        enc_grad,
        dec_grad,
        att_in,
        att_in_bias,
        att_out,
        att_out_bias,
        ffn_in,
        ffn_in_bias,
        ffn_out,
        ffn_out_bias,
        gain,
        shift,
        rms,
    )


def solution(mesh):
    rows = P((DP, TENSOR), None)
    placed = (
        rows,
        rows,
        P(DP, None),
        P(DP, None, TENSOR, None),
        P(None, None, TENSOR),
        P(None, TENSOR),
        P(None, None, TENSOR),
        P(),
        P(None, None, TENSOR),
        P(None, TENSOR),
        P(None, None, TENSOR),
        P(),
        P(),
        P(),
        rows,
    )
    split = P(None, DP, TENSOR)
    return jax.shard_map(
        functools.partial(body, mesh.shape[DP]),
        mesh=mesh,
        in_specs=placed,
        out_specs=(rows, rows, rows, split, P(), split, P(), split, P(), split, P(), P(), P(), P()),
        check_vma=False,
    )
```

```python
import functools
from types import SimpleNamespace
from typing import Any, NamedTuple

import jax
import jax.numpy as jnp
from jax import lax
from jax.experimental import pallas as pl
from jax.experimental.pallas import tpu as pltpu
from jax.sharding import PartitionSpec as P

HEAD = 64
EPS = 1e-05
NEG = -1e30
MESH = pl.DeviceIdType.MESH
DP, TENSOR = "dp", "tensor"
PROBS, ALL_GRADS = "probs", "grads"
F32 = jnp.float32
BF16 = jnp.bfloat16

ROW_ATT_OUT_BIAS = 0
ROW_FFN_OUT_BIAS = 3
ROW_GAIN = 5
ROW_SHIFT = 10
ROW_SQUARE = 15
ROW_FFN_IN_BIAS = 24
ROW_ATT_IN_BIAS = 30
SUM_ROWS = 40
LATE_ROWS = 8
LATE_NORM_ROWS = 3

ATT, FFN_IN, FFN_OUT = range(3)
GRADS = (
    (FFN_OUT, 1, (2, 1, 4), 0, 0, 2),
    (FFN_OUT, 1, (1, 2, 4), 0, 2, 4),
    (FFN_IN, 1, (2, 1, 4), 1, 0, 2),
    (FFN_IN, 1, (1, 2, 4), 1, 2, 4),
    (ATT, 2, (2, 1, 4), 2, 0, 2),
    (ATT, 2, (1, 4, 2), 2, 2, 4),
    (ATT, 1, (1, 4, 2), 4, 0, 2),
    (ATT, 1, (2, 1, 4), 4, 2, 4),
    (FFN_OUT, 0, (1, 4, 2), 3, 0, 2),
    (FFN_OUT, 0, (1, 2, 4), 3, 2, 4),
    (FFN_IN, 0, (2, 1, 4), 0, 0, 2),
    (FFN_IN, 0, (1, 2, 4), 0, 2, 4),
    (ATT, 0, (1, 2, 4), 1, 0, 2),
    (ATT, 0, (1, 2, 4), 1, 2, 4),
)
SLOTS = 5
WHOLE = tuple(grad[:2] for grad in GRADS if grad[4] == 0)


def next_in_slot(k):
    later = range(k + 1, len(GRADS))
    return [j for j in later if GRADS[j][3:] == GRADS[k][3:]]


def waits_for_slot(k):
    return any(k in next_in_slot(j) for j in range(k))


def mm(left, right):
    return jnp.dot(left, right, preferred_element_type=F32)


def mm_nt(left, right):
    return lax.dot_general(left, right, (((1,), (1,)), ((), ())), preferred_element_type=F32)


def mm_tn(left, right):
    return lax.dot_general(left, right, (((0,), (0,)), ((), ())), preferred_element_type=F32)


def bit_of(value, bit):
    return lax.rem(lax.div(value, jnp.int32(bit)), jnp.int32(2))


def flipped(value, bit):
    return value + bit - 2 * bit * bit_of(value, bit)


def column_sum(values):
    return jnp.sum(values, axis=0, keepdims=True)


class Inputs(NamedTuple):
    enc_input: Any
    dec_input: Any
    segment_ids: Any
    retrieval: Any
    att_in: Any
    att_in_bias: Any
    att_out: Any
    att_out_bias: Any
    ffn_in: Any
    ffn_in_bias: Any
    ffn_out: Any
    ffn_out_bias: Any
    ln_gain: Any
    ln_bias: Any
    d_out: Any


IN_HBM = Inputs(
    enc_input=True,
    dec_input=True,
    segment_ids=False,
    retrieval=True,
    att_in=True,
    att_in_bias=False,
    att_out=True,
    att_out_bias=False,
    ffn_in=True,
    ffn_in_bias=False,
    ffn_out=True,
    ffn_out_bias=False,
    ln_gain=False,
    ln_bias=False,
    d_out=True,
)


class Plan:
    def __init__(self, args, n_dp):
        self.D = D = args.enc_input.shape[1]
        self.CE = CE = args.enc_input.shape[0]
        self.HD = HD = args.dec_input.shape[0]
        self.HE = HE = CE // 2
        self.CD = 2 * HD
        self.R = R = 4 * CE
        self.S = S = 4 * HD
        self.A = A = args.att_in.shape[1]
        self.heads = heads = A // HEAD
        self.F = F = args.ffn_in.shape[2]
        self.picks = args.retrieval.shape[3]
        self.inside = n_dp == 8
        self.block = D // 8
        self.scratch = {}
        self.n_sems = 0
        self.at = SimpleNamespace()

        wide = ((R, D), BF16)
        short = ((S, D), BF16)
        enc_heads = ((R, A), BF16)
        dec_heads = ((S, A), BF16)
        enc_float = ((4, HE, D), F32)
        dec_float = ((2, HD, D), F32)
        enc_half = ((4, HE, D), BF16)
        dec_half = ((2, HD, D), BF16)
        enc_column = ((4, HE, 1), F32)
        dec_column = ((2, HD, 1), F32)
        stacked = ((heads * CE, A), BF16)
        self.vmem(
            ATI=((9, A, D), BF16),
            ATO=((3, A, D), BF16),
            FFI=((D, F), BF16),
            FFO=((D, F), BF16),
            RET=((heads, S, self.picks), jnp.int32),
        )
        self.vmem(X=wide, H1=wide, MEM=wide, E2=wide)
        self.vmem(DX=short, G1=short, G2=short, E5=short, E4=short)
        self.vmem(DOU=dec_half, G3S=dec_half)
        self.vmem(Q=enc_heads, K=enc_heads, V=enc_heads, O=enc_heads)
        self.vmem(K2=enc_heads, V2=enc_heads)
        turned = ((A, R), BF16)
        self.vmem(KT=turned, VT=turned, VT2=turned)
        self.vmem(KTD=((A, S), BF16), VTD=((A, S), BF16))
        self.vmem(QD=dec_heads, KD=dec_heads, VD=dec_heads, OD=dec_heads, UPD=dec_heads)
        self.vmem(Q2=dec_heads, O2=dec_heads)
        self.vmem(DK=((A, R), F32), DV=((A, R), F32))
        self.vmem(BIG=((3, heads * CE, R), BF16), PD=((heads * S, S), BF16), QS=stacked, DOS=stacked)
        self.vmem(ACT0=((R, F), BF16), GP0=((R, F), BF16), ACT1=((S, F), BF16), GP1=((S, F), BF16))
        self.vmem(XH0=enc_float, XH1=enc_float, RES=enc_float)
        self.vmem(XH2=dec_float, XH3=dec_float, XH4=dec_float, RESD=dec_float)
        self.vmem(RS0=enc_column, RS1=enc_column, RS2=dec_column, RS3=dec_column, RS4=dec_column)
        self.vmem(SEGR=((1, R), F32), SEGC=((R, 1), F32), T=((D, R), BF16))
        self.vmem(OWN=((HE, D), F32), OWND=((HD, D), F32))
        self.vmem(PR=enc_half, PS=enc_half, XS=enc_half, XR=((2, 4, HE, D), BF16))
        self.vmem(PRD=dec_half, PSD=dec_half, XSD=dec_half, XRD=((2, 2, HD, D), BF16))
        self.vmem(GR=((SLOTS, 8, self.block, D), BF16))
        if self.inside:
            self.vmem(
                R1=((SLOTS, 4, self.block, D), BF16),
                R2=((SLOTS, 2, self.block, D), BF16),
                R3=((SLOTS, 1, self.block, D), BF16),
                SUMR=((5, SUM_ROWS, D), F32),
                LATR=((5, LATE_ROWS, D), F32),
            )
        self.vmem(SUM=((SUM_ROWS, D), F32), LATE=((LATE_ROWS, D), F32))
        self.vmem(GAIN=((5, D), F32), SHIFT=((5, D), F32))
        self.vmem(AIB=((6, A), F32), AOB=((3, D), F32), FIB=((2, F), F32), FOB=((2, D), F32))
        self.sem(load=8, own=4, ag=24, pst=2, enc=24, dec=12)
        self.sem(H1=8, MEM=8, E2=8, E1=8, G1=4, G2=4, E5=4, E4=4, E3=4)
        self.sem(grad=84, sum=30)

    def vmem(self, **buffers):
        for name, (shape, dtype) in buffers.items():
            self.scratch[name] = pltpu.VMEM(shape, dtype)

    def sem(self, **counts):
        for name, count in counts.items():
            setattr(self.at, name, self.n_sems)
            self.n_sems += count


class Outputs(NamedTuple):
    dec_output: Any
    enc_grad: Any
    dec_grad: Any
    sums: Any
    late: Any
    probs: Any
    grads: Any = None
    att_in: Any = None
    att_out: Any = None
    ffn_in: Any = None
    ffn_out: Any = None


def kernel(p, made, *refs):
    n_in = len(Inputs._fields)
    ins = Inputs(*refs[:n_in])
    outs = Outputs(*[None if index is None else refs[n_in + index] for index in made])
    n_out = sum(index is not None for index in made)
    b = SimpleNamespace(**dict(zip(p.scratch, refs[n_in + n_out : -2])))
    sems, free = refs[-2:]
    b.CNT, b.DS = b.BIG.at[1], b.BIG.at[2]
    b.KT2, b.UP, b.E3, b.D2 = b.KT, b.K2, b.E5, b.Q2
    D, A, F, R, S, CE, HE, CD, HD = p.D, p.A, p.F, p.R, p.S, p.CE, p.HE, p.CD, p.HD
    heads, at = p.heads, p.at
    block_rows = 128

    t = lax.axis_index(TENSOR)
    dp = lax.axis_index(DP)
    x, c = lax.div(t, jnp.int32(2)), lax.rem(t, jnp.int32(2))
    pair = (dp, t + 1 - 2 * c)
    across = (dp, t + 2 - 4 * x)

    def sem(base, index):
        return sems.at[base + index]

    def remote(src, dst, base, index, target):
        return pltpu.make_async_remote_copy(
            src_ref=src,
            dst_ref=dst,
            send_sem=sem(base, 2 * index),
            recv_sem=sem(base, 2 * index + 1),
            device_id=target,
            device_id_type=MESH,
        )

    partners = [pair, across]
    if p.inside:
        partners += [(flipped(dp, bit), t) for bit in (1, 2, 4)]
    barrier = pltpu.get_barrier_semaphore()
    for partner in partners:
        pl.semaphore_signal(barrier, inc=1, device_id=partner, device_id_type=MESH)

    loads = [
        pltpu.make_async_copy(ins.retrieval.at[0], b.RET, sem(at.load, 0)),
        pltpu.make_async_copy(ins.att_in, b.ATI, sem(at.load, 1)),
        pltpu.make_async_copy(ins.att_out, b.ATO, sem(at.load, 2)),
    ]
    for copy in loads:
        copy.start()

    def load_ffn(f):
        return (
            pltpu.make_async_copy(ins.ffn_in.at[f], b.FFI, sem(at.load, 3)),
            pltpu.make_async_copy(ins.ffn_out.at[f], b.FFO, sem(at.load, 4)),
        )

    for copy in load_ffn(0):
        copy.start()

    pl.semaphore_wait(barrier, len(partners))

    def place(owner_x, owner_c, half):
        return pl.ds(pl.multiple_of((2 * owner_x + half) * CE + owner_c * HE, HE), HE)

    def enc_copy(half, target, index):
        src = ins.enc_input.at[pl.ds(half * HE, HE)]
        return remote(src, b.X.at[place(x, c, half)], at.ag, index, target)

    def enc_forward(half, index):
        rows = place(1 - x, c, half)
        return remote(b.X.at[rows], b.X.at[rows], at.ag, index, pair)

    dec_rows = pl.ds(pl.multiple_of(t * HD, HD), HD)
    far_rows = pl.ds(pl.multiple_of((t + 2 - 4 * x) * HD, HD), HD)

    def dec_copy(target, index):
        return remote(ins.dec_input, b.DX.at[dec_rows], at.ag, index, target)

    def dec_forward(index):
        return remote(b.DX.at[far_rows], b.DX.at[far_rows], at.ag, index, pair)

    ag_x = [enc_copy(0, across, 0), enc_copy(1, across, 1), dec_copy(across, 2)]
    ag_x.append(remote(ins.d_out, b.DOU.at[x], at.ag, 3, across))
    ag_p = [enc_copy(0, pair, 4), enc_copy(1, pair, 5), dec_copy(pair, 6)]
    ag_f = [enc_forward(0, 7), enc_forward(1, 8), dec_forward(9)]
    for copy in ag_x + ag_p:
        copy.start()
    own_copies = [
        pltpu.make_async_copy(
            ins.enc_input.at[pl.ds(0, HE)], b.X.at[place(x, c, 0)], sem(at.own, 0)
        ),
        pltpu.make_async_copy(
            ins.enc_input.at[pl.ds(HE, HE)], b.X.at[place(x, c, 1)], sem(at.own, 1)
        ),
        pltpu.make_async_copy(ins.dec_input, b.DX.at[dec_rows], sem(at.own, 2)),
        pltpu.make_async_copy(ins.d_out, b.DOU.at[x], sem(at.own, 3)),
    ]
    for copy in own_copies:
        copy.start()

    b.GAIN[...] = ins.ln_gain[...].astype(F32)
    b.SHIFT[...] = ins.ln_bias[...].astype(F32)
    b.AIB[...] = ins.att_in_bias[...].astype(F32)
    b.AOB[...] = ins.att_out_bias[...].astype(F32)
    b.FIB[...] = ins.ffn_in_bias[...].astype(F32)
    b.FOB[...] = ins.ffn_out_bias[...].astype(F32)
    b.SUM[...] = jnp.zeros((SUM_ROWS, D), F32)
    b.LATE[...] = jnp.zeros((LATE_ROWS, D), F32)
    segments = ins.segment_ids[...].astype(F32)
    order = (0, 2, 1, 3, 4, 6, 5, 7)
    pieces = [segments[:, HE * o : HE * (o + 1)] for o in order]
    b.SEGR[...] = jnp.concatenate(pieces, axis=1)
    standing = jnp.concatenate(pieces, axis=0).T
    for k in range(8):
        b.SEGC[HE * k : HE * (k + 1), :] = standing[:, k : k + 1]

    lane_head = lax.broadcasted_iota(jnp.int32, (1, A), 1) // HEAD
    head_masks = [lane_head == h for h in range(heads)]
    zero16 = jnp.zeros((), BF16)

    def only_head(values, h):
        return jnp.where(head_masks[h], values, zero16)

    loads[0].wait()
    lanes = p.picks

    def count_block(index, carry):
        base = pl.multiple_of(index * 16, 16)
        block = lax.div(index, jnp.int32(block_rows // 16))
        within = lax.rem(index, jnp.int32(block_rows // 16)) * 16
        first = pl.multiple_of(block * (heads * block_rows) + within, 16)
        for h in range(heads):
            halves = []
            for part in range(2):
                picks = b.RET[h, pl.ds(base + 8 * part, 8), :]
                high = lax.shift_right_logical(picks, 7)
                low = picks & 127
                swapped = (high & 4) | ((high & 1) << 1) | ((high >> 1) & 1)
                code = swapped * 8 + lax.broadcasted_iota(jnp.int32, (8, lanes), 0)
                codes = lax.broadcasted_iota(jnp.int32, (64, lanes), 0)
                lows = lax.broadcasted_iota(jnp.int32, (128, lanes), 0)
                left = jnp.concatenate(
                    [jnp.where(codes == code[k : k + 1, :], 1.0, 0.0).astype(BF16) for k in range(8)],
                    axis=1,
                )
                right = jnp.concatenate(
                    [jnp.where(lows == low[k : k + 1, :], 1.0, 0.0).astype(BF16) for k in range(8)],
                    axis=1,
                )
                halves.append(mm_nt(left, right))
            for k in range(8):
                value = jnp.concatenate([half[8 * k : 8 * k + 8] for half in halves], axis=0)
                b.CNT[pl.ds(first + h * block_rows, 16), 128 * k : 128 * (k + 1)] = value.astype(BF16)
        return carry

    def project(source, rows, index, target_q, target_k, target_v, turned_k, turned_v):
        if target_q is not None:
            bias = b.AIB[2 * index : 2 * index + 1, :]
            value = (mm_nt(source, b.ATI[3 * index]) + bias).astype(BF16)
            target_q[rows, :] = value * jnp.asarray(0.125, BF16)
        if target_k is not None:
            value = mm_nt(source, b.ATI[3 * index + 1]).astype(BF16)
            target_k[rows, :] = value
            turned_k[:, rows] = value.T
            bias = b.AIB[2 * index + 1 : 2 * index + 2, :]
            value = (mm_nt(source, b.ATI[3 * index + 2]) + bias).astype(BF16)
            target_v[rows, :] = value
            turned_v[:, rows] = value.T

    def enc_rows(i):
        if isinstance(i, int):
            return slice(i * CE, (i + 1) * CE)
        return pl.ds(pl.multiple_of(i * CE, CE), CE)

    def dec_chunk(i):
        return pl.ds(pl.multiple_of(i * CD, CD), CD)

    def enc_mine(i):
        return pl.ds(pl.multiple_of(i * CE + c * HE, HE), HE)

    def dec_mine(i):
        return pl.ds(pl.multiple_of(i * CD + c * HD, HD), HD)

    def enc_sum(k):
        s = k % 2

        def pair_copy(i):
            return remote(b.PS.at[i], b.PR.at[i], at.enc, i, pair)

        def across_copy(i):
            return remote(b.XS.at[i], b.XR.at[s, i], at.enc, 4 + 4 * s + i, across)

        return (pair_copy, across_copy, b.OWN, b.PS, b.XS, b.PR, b.XR.at[s], HE)

    def dec_sum(k):
        s = k % 2

        def pair_copy(i):
            return remote(b.PSD.at[i], b.PRD.at[i], at.dec, i, pair)

        def across_copy(i):
            return remote(b.XSD.at[i], b.XRD.at[s, i], at.dec, 2 + 2 * s + i, across)

        return (
            pair_copy,
            across_copy,
            b.OWND,
            b.PSD,
            b.XSD,
            b.PRD,
            b.XRD.at[s],
            HD,
        )

    def pair_send(group, i, part):
        pair_copy, _, own, sent, _, _, _, half = group
        first, second = part[:half], part[half:]
        own[...] = jnp.where(c == 0, first, second)
        sent[i] = jnp.where(c == 0, second, first).astype(BF16)
        pair_copy(i).start()

    def pair_take(group, i):
        pair_copy, _, own, _, _, got, _, _ = group
        copy = pair_copy(i)
        copy.wait()
        return own[...] + got[i].astype(F32)

    def across_prepare(group, i):
        sent = group[4]
        sent[i] = pair_take(group, i).astype(BF16)

    def across_start(group, i):
        group[1](i).start()

    def across_send(group, i):
        across_prepare(group, i)
        across_start(group, i)

    def across_take(group, i):
        _, across_copy, _, _, sent, _, got, _ = group
        across_copy(i).wait()
        return sent[i].astype(F32) + got[i].astype(F32)

    def gather_copy(base, target, rows, i):
        return remote(target.at[rows], target.at[rows], base, i, pair)

    def gather_start(base, target, rows, i, value):
        target[rows, :] = value
        gather_copy(base, target, rows, i).start()

    def norm(index, value, xhat_ref, rstd_ref, i):
        center = value - jnp.mean(value, axis=-1, keepdims=True)
        rstd = lax.rsqrt(jnp.mean(center * center, axis=-1, keepdims=True) + EPS)
        xhat = center * rstd
        xhat_ref[i] = xhat
        rstd_ref[i] = rstd
        return xhat * b.GAIN[index : index + 1, :] + b.SHIFT[index : index + 1, :]

    def add_sum(row, value):
        b.SUM[row : row + 1, :] += column_sum(value)

    def norm_back(index, dy, xhat_ref, rstd_ref, i, bias_row):
        xhat = xhat_ref[i]
        scaled = dy * b.GAIN[index : index + 1, :]
        mean = jnp.mean(scaled, axis=-1, keepdims=True)
        along = jnp.mean(scaled * xhat, axis=-1, keepdims=True)
        dz = (scaled - mean - xhat * along) * rstd_ref[i]
        if index == 0:
            for row, value in enumerate((dz, dy * xhat, dy)):
                b.LATE[row : row + 1, :] += column_sum(value)
            return dz
        add_sum(ROW_GAIN + index, dy * xhat)
        add_sum(ROW_SHIFT + index, dy)
        add_sum(bias_row, dz)
        return dz

    def branch_of(total, bias, square):
        branch = total + bias
        add_sum(ROW_SQUARE + square, branch * branch)
        return branch

    def feed(rows, source, index, act_ref, slope_ref):
        for first in range(0, F, 256):
            cols = slice(first, first + 256)
            before = mm(source, b.FFI[:, cols]) + b.FIB[index : index + 1, cols]
            share = 0.5 + 0.5 * lax.erf(before * 0.7071067811865476)
            slope = share + before * jnp.exp(before * before * -0.5) * 0.3989422804014327
            act_ref[rows, cols] = (before * share).astype(BF16)
            slope_ref[rows, cols] = slope.astype(BF16)
        return mm_nt(act_ref[rows, :], b.FFO[...])

    def feed_back(rows, upstream, slope_ref):
        for first in range(0, F, 256):
            cols = slice(first, first + 256)
            dact = mm(upstream, b.FFO[:, cols])
            slope_ref[rows, cols] = (dact * slope_ref[rows, cols].astype(F32)).astype(BF16)
        return mm_nt(slope_ref[rows, :], b.FFI[...])

    def project_enc(i):
        rows = enc_rows(i)
        project(b.X[rows, :], rows, 0, b.Q, b.K, b.V, b.KT, b.VT)

    for copy in own_copies[:3]:
        copy.wait()
    loads[1].wait()
    loads[2].wait()
    ag_p[0].wait_recv()
    project_enc(2 * x)
    ag_p[1].wait_recv()
    project_enc(2 * x + 1)
    lax.fori_loop(0, 4, count_block, 0)
    ag_x[0].wait_recv()
    ag_f[0].start()
    lax.fori_loop(4, 8, count_block, 0)
    ag_x[1].wait_recv()
    ag_f[1].start()
    ag_f[0].wait_recv()
    project_enc(2 - 2 * x)
    ag_f[1].wait_recv()
    project_enc(3 - 2 * x)

    def p_store(i):
        slot = i % 2 if isinstance(i, int) else lax.rem(i, jnp.int32(2))
        return pltpu.make_async_copy(b.BIG.at[2 * slot], outs.probs.at[i], sem(at.pst, slot))

    def p_load(i):
        slot = i % 2 if isinstance(i, int) else lax.rem(i, jnp.int32(2))
        return pltpu.make_async_copy(outs.probs.at[i], b.BIG.at[slot], sem(at.pst, slot))

    stack = heads * block_rows

    def heads_stacked(values):
        return jnp.concatenate([only_head(values, h) for h in range(heads)], axis=0)

    def heads_joined(values):
        joined = values[:block_rows]
        for h in range(1, heads):
            own = values[h * block_rows : (h + 1) * block_rows]
            joined = jnp.where(head_masks[h], own, joined)
        return joined

    def attend(q, kt_ref, v_ref, p_ref, first, same):
        scores = mm(heads_stacked(q), kt_ref[...])
        for h in range(heads):
            rows = pl.ds(pl.multiple_of(first + h * block_rows, block_rows), block_rows)
            own = scores[h * block_rows : (h + 1) * block_rows]
            if same is None:
                weight = p_ref[rows, :].astype(F32)
                own = jnp.where(weight > 0, own, NEG)
                expo = weight * jnp.exp(own - jnp.max(own, axis=-1, keepdims=True))
            else:
                own = jnp.where(same, own, NEG)
                expo = jnp.exp(own - jnp.max(own, axis=-1, keepdims=True))
            scale = 1.0 / jnp.sum(expo, axis=-1, keepdims=True)
            p_ref[rows, :] = (expo * scale).astype(BF16)
        probs = p_ref[pl.ds(pl.multiple_of(first, block_rows), stack), :]
        return heads_joined(mm(probs, v_ref[...])).astype(BF16)

    sum0 = enc_sum(0)

    def att_fwd(i, carry):
        slot = lax.rem(i, jnp.int32(2))

        @pl.when(i >= 2)
        def _():
            p_store(i - 2).wait()

        @pl.when(i == 2)
        def _():
            ag_x[2].wait_recv()
            ag_f[2].start()

        def one_block(index, carry):
            own = pl.ds(pl.multiple_of(i * CE + index * block_rows, block_rows), block_rows)
            same = b.SEGC[own, :] == b.SEGR[...]
            p_ref = b.BIG.at[2 * slot]
            b.O[own, :] = attend(b.Q[own, :], b.KT, b.V, p_ref, index * stack, same)

            @pl.when((index == 0) & (i > 0))
            def _():
                across_send(sum0, i - 1)

            return carry

        lax.fori_loop(0, CE // block_rows, one_block, 0)
        p_store(i).start()
        pair_send(sum0, i, mm(b.O[enc_rows(i), :], b.ATO[0]))
        return carry

    lax.fori_loop(0, 4, att_fwd, 0)

    dsum0 = dec_sum(0)
    whole = pl.ds(0, S)
    ag_p[2].wait_recv()
    ag_f[2].wait_recv()
    project(b.DX[...], whole, 1, b.QD, b.KD, b.VD, b.KTD, b.VTD)
    across_send(sum0, 3)
    p_store(2).wait()
    p_store(3).wait()

    def dec_fwd(i, carry):
        rows = dec_chunk(i)
        row_index = lax.broadcasted_iota(jnp.int32, (CD, S), 0) + i * CD
        keep = row_index >= lax.broadcasted_iota(jnp.int32, (CD, S), 1)
        joined = attend(b.QD[rows, :], b.KTD, b.VD, b.PD, i * stack, keep)
        b.OD[rows, :] = joined
        pair_send(dsum0, i, mm(joined, b.ATO[1]))
        across_send(dsum0, i)
        return carry

    lax.fori_loop(0, 2, dec_fwd, 0)

    sum1 = enc_sum(1)
    for copy in load_ffn(0):
        copy.wait()

    def ffn_fwd(i, carry):
        mine = enc_mine(i)
        branch = branch_of(across_take(sum0, i), b.AOB[0:1, :], 0)
        hidden = norm(0, b.X[mine, :].astype(F32) + branch, b.XH0, b.RS0, i)
        b.RES[i] = hidden
        gather_start(at.H1, b.H1, mine, i, hidden.astype(BF16))
        count_block(8 + 2 * i, 0)
        gather_copy(at.H1, b.H1, mine, i).wait()
        rows = enc_rows(i)
        pair_send(sum1, i, feed(rows, b.H1[rows, :], 0, b.ACT0, b.GP0))
        count_block(9 + 2 * i, 0)
        across_send(sum1, i)
        return carry

    lax.fori_loop(0, 4, ffn_fwd, 0)
    for copy in load_ffn(1):
        copy.start()

    def dec_norm(i, carry):
        mine = dec_mine(i)
        branch = branch_of(across_take(dsum0, i), b.AOB[1:2, :], 2)
        hidden = norm(2, b.DX[mine, :].astype(F32) + branch, b.XH2, b.RS2, i)
        b.RESD[i] = hidden
        gather_start(at.G1, b.G1, mine, i, hidden.astype(BF16))
        return carry

    lax.fori_loop(0, 2, dec_norm, 0)
    for i in range(2):
        gather_copy(at.G1, b.G1, dec_mine(i), i).wait()
    project(b.G1[...], whole, 2, b.Q2, None, None, None, None)

    def memory_fwd(i, carry):
        mine = enc_mine(i)
        branch = branch_of(across_take(sum1, i), b.FOB[0:1, :], 1)
        hidden = norm(1, b.RES[i] + branch, b.XH1, b.RS1, i)
        add_sum(ROW_SQUARE + 5, hidden * hidden)
        gather_start(at.MEM, b.MEM, mine, i, hidden.astype(BF16))
        gather_copy(at.MEM, b.MEM, mine, i).wait()
        rows = enc_rows(i)
        project(b.MEM[rows, :], rows, 2, None, b.K2, b.V2, b.KT2, b.VT2)
        return carry

    lax.fori_loop(0, 4, memory_fwd, 0)

    dsum1 = dec_sum(1)

    def cross_fwd(i, carry):
        rows = dec_chunk(i)
        joined = attend(b.Q2[rows, :], b.KT2, b.V2, b.CNT, i * stack, None)
        b.O2[rows, :] = joined
        pair_send(dsum1, i, mm(joined, b.ATO[2]))
        across_send(dsum1, i)
        return carry

    lax.fori_loop(0, 2, cross_fwd, 0)
    for copy in load_ffn(1):
        copy.wait()

    dsum2 = dec_sum(2)

    def dec_feed(i, carry):
        mine = dec_mine(i)
        branch = branch_of(across_take(dsum1, i), b.AOB[2:3, :], 3)
        hidden = norm(3, b.RESD[i] + branch, b.XH3, b.RS3, i)
        b.RESD[i] = hidden
        gather_start(at.G2, b.G2, mine, i, hidden.astype(BF16))
        gather_copy(at.G2, b.G2, mine, i).wait()
        rows = dec_chunk(i)
        pair_send(dsum2, i, feed(rows, b.G2[rows, :], 1, b.ACT1, b.GP1))
        across_send(dsum2, i)
        return carry

    lax.fori_loop(0, 2, dec_feed, 0)

    dsum3 = dec_sum(3)
    ag_x[3].wait_recv()
    own_copies[3].wait()

    def dec_turn(i, carry):
        mine = dec_mine(i)
        branch = branch_of(across_take(dsum2, i), b.FOB[1:2, :], 4)
        hidden = norm(4, b.RESD[i] + branch, b.XH4, b.RS4, i)
        add_sum(ROW_SQUARE + 6, hidden * hidden)
        b.G3S[i] = hidden.astype(BF16)
        dy = b.DOU[i].astype(F32)
        dz = norm_back(4, dy, b.XH4, b.RS4, i, ROW_FFN_OUT_BIAS + 1)
        b.RESD[i] = dz
        gather_start(at.E5, b.E5, mine, i, dz.astype(BF16))
        gather_copy(at.E5, b.E5, mine, i).wait()
        rows = dec_chunk(i)
        pair_send(dsum3, i, feed_back(rows, b.E5[rows, :], b.GP1))
        across_send(dsum3, i)
        return carry

    lax.fori_loop(0, 2, dec_turn, 0)
    outs.dec_output[...] = b.G3S[x]
    for copy in load_ffn(0):
        copy.start()

    def grad_place(k, j):
        if not p.inside:
            return j
        first, second, third = GRADS[k][2]
        return (j // first % 2) * 4 + (j // second % 2) * 2 + (j // third % 2)

    def transpose_into(source, rows):
        step = min(rows, 256)
        for first in range(0, rows, step):
            b.T[:, first : first + step] = source[first : first + step, :].T

    def grad_columns(half, rows, right, first):
        slot = GRADS[half][3]
        quarter = D // 2
        count = right.shape[1]
        for a in range(2):
            value = mm(b.T[a * quarter : (a + 1) * quarter, :rows], right[...]).astype(BF16)
            for k in (half, half + 1):
                low, high = max(first, GRADS[k][4] * A), min(first + count, GRADS[k][5] * A)
                for jj in range(4 if low < high else 0):
                    where = grad_place(k, 4 * a + jj)
                    rows_own = slice(jj * p.block, (jj + 1) * p.block)
                    b.GR[slot, where, :, low:high] = value[rows_own, low - first : high - first]

    def grad_copy(k, step):
        _, _, bits, slot, low, high = GRADS[k]
        cols = pl.ds(low * A, (high - low) * A)
        if not p.inside:
            whole_index = WHOLE.index(GRADS[k][:2])
            return pltpu.make_async_copy(b.GR.at[slot], outs.grads.at[whole_index], sem(at.grad, k))
        target = (flipped(dp, bits[step]), t)
        mine = [bit_of(dp, bit) for bit in bits]
        if step == 0:
            first, count, got = 4 * (1 - mine[0]), 4, b.R1
        elif step == 1:
            first, count, got = 4 * mine[0] + 2 * (1 - mine[1]), 2, b.R2
        else:
            first, count, got = 4 * mine[0] + 2 * mine[1] + 1 - mine[2], 1, b.R3
        src = b.GR.at[slot, pl.ds(first, count), :, cols]
        return remote(src, got.at[slot, :, :, cols], at.grad, 3 * k + step, target)

    def grad_step(k, step):
        kind, index, bits, slot, low, high = GRADS[k]
        if not p.inside:
            if high == 4 and step == 0:
                grad_copy(k, 0).start()
            if high == 4 and step == 3:
                grad_copy(k, 0).wait()
            return
        cols = slice(low * A, high * A)
        mine = [bit_of(dp, bit) for bit in bits]
        if step > 0:
            grad_copy(k, step - 1).wait()
        if step in (1, 2):
            got = b.R1 if step == 1 else b.R2
            base = 4 * mine[0] if step == 1 else 4 * mine[0] + 2 * mine[1]
            for j in range(got.shape[1]):
                total = b.GR[slot, base + j, :, cols].astype(F32) + got[slot, j, :, cols].astype(F32)
                b.GR[slot, base + j, :, cols] = total.astype(BF16)
        if step == 3:
            place_own = 4 * mine[0] + 2 * mine[1] + mine[2]
            total = b.GR[slot, place_own, :, cols].astype(F32) + b.R3[slot, 0, :, cols].astype(F32)
            if kind == ATT:
                for j in range(low, high):
                    part = total[:, (j - low) * A : (j - low + 1) * A]
                    if j < 3:
                        outs.att_in[3 * index + j] = part
                    else:
                        outs.att_out[index] = part
            elif kind == FFN_IN:
                outs.ffn_in[index, :, cols] = total
            else:
                outs.ffn_out[index, :, cols] = total
        if step > 0:
            for j in next_in_slot(k):
                later = (flipped(dp, GRADS[j][2][step - 1]), t)
                free_sem = free.at[3 * j + step - 1]
                pl.semaphore_signal(free_sem, inc=1, device_id=later, device_id_type=MESH)
        if step < 3:
            if waits_for_slot(k):
                pl.semaphore_wait(free.at[3 * k + step], 1)
            grad_copy(k, step).start()

    def ffn_in_bias(f, dpre_ref):
        def gather_rows(i, total):
            block = dpre_ref[pl.ds(pl.multiple_of(i * CD, CD), CD), :]
            return total + column_sum(block.astype(F32))

        total = lax.fori_loop(0, dpre_ref.shape[0] // CD, gather_rows, jnp.zeros((1, F), F32))
        for owner in range(4):
            row = ROW_FFN_IN_BIAS + 4 * f + owner
            b.SUM[row : row + 1, :] = jnp.where(t == owner, total, 0.0)

    def att_bias(index, dq_ref, dv_ref):
        rows = []
        for ref in (dq_ref, dv_ref):
            rows.append(column_sum(ref[...].astype(F32)))
        table, first = (b.LATE, LATE_NORM_ROWS) if index == 0 else (b.SUM, ROW_ATT_IN_BIAS + 2 * index)
        for owner in range(4):
            for j in range(2):
                cols = slice(owner * A, (owner + 1) * A)
                table[first + j : first + j + 1, cols] = jnp.where(t == owner, rows[j], 0.0)

    def decoder_ffn_out_grad():
        transpose_into(b.E5, S)
        grad_columns(0, S, b.ACT1, 0)

    def decoder_ffn_in_grad():
        transpose_into(b.G2, S)
        grad_columns(2, S, b.GP1, 0)

    def attention_back(up_ref, q_ref, o_ref, first, k_ref, vt_ref, p_ref, d_ref, count, span):
        def one_block(index):
            own = pl.ds(pl.multiple_of(first + index * block_rows, block_rows), block_rows)
            stacked = slice(index * stack, (index + 1) * stack)
            upstream = up_ref[own, :]
            along = upstream.astype(F32) * o_ref[own, :].astype(F32)
            ups = heads_stacked(upstream)
            b.DOS[stacked, :] = ups
            b.QS[stacked, :] = heads_stacked(q_ref[own, :])
            dprobs = mm(ups, vt_ref[...])
            for h in range(heads):
                rows = slice(index * stack + h * block_rows, index * stack + (h + 1) * block_rows)
                inner = jnp.sum(jnp.where(head_masks[h], along, 0.0), axis=-1, keepdims=True)
                part = dprobs[h * block_rows : (h + 1) * block_rows] - inner
                b.DS[rows, :span] = (p_ref[rows, :].astype(F32) * part).astype(BF16)
            dq = heads_joined(mm(b.DS[stacked, :span], k_ref[...]))
            d_ref[own, :] = (dq * 0.125).astype(BF16)

        for index in range(count // block_rows):
            one_block(index)

    dsum4 = dec_sum(4)
    sum2 = enc_sum(2)
    sum3 = enc_sum(3)
    dsum5 = dec_sum(5)
    sum4 = enc_sum(4)

    def send_two(group, first, second, part_of):
        pair_send(group, first, part_of(first))
        part = part_of(second)
        across_send(group, first)
        pair_send(group, second, part)
        across_send(group, second)

    def cross_back():
        ffn_in_bias(1, b.GP1)
        for i in range(2):
            mine = dec_mine(i)
            dy = b.RESD[i] + across_take(dsum3, i)
            dz = norm_back(3, dy, b.XH3, b.RS3, i, ROW_ATT_OUT_BIAS + 2)
            b.RESD[i] = dz
            gather_start(at.E4, b.E4, mine, i, dz.astype(BF16))
        for i in range(2):
            gather_copy(at.E4, b.E4, dec_mine(i), i).wait()
        b.UPD[...] = mm_nt(b.E4[...], b.ATO[2]).astype(BF16)
        attention_back(b.UPD, b.Q2, b.O2, jnp.int32(0), b.K2, b.VT2, b.CNT, b.D2, S, R)
        for i in range(4):
            cols = slice(i * CE, (i + 1) * CE)
            b.K2[cols, :] = mm_tn(b.QS[: heads * S, :], b.DS[: heads * S, cols]).astype(BF16).T
            b.V2[cols, :] = mm_tn(b.DOS[: heads * S, :], b.CNT[:, cols]).astype(BF16).T
        att_bias(2, b.D2, b.V2)

    def memory_part(i):
        rows = slice(i * CE, (i + 1) * CE)
        return mm(b.K2[rows, :], b.ATI[7]) + mm(b.V2[rows, :], b.ATI[8])

    def query_part(i):
        return mm(b.D2[i * CD : (i + 1) * CD, :], b.ATI[6])

    def cross_grad(half):
        if half == 0:
            transpose_into(b.G1, S)
            grad_columns(4, S, b.D2, 0)
            transpose_into(b.MEM, R)
            grad_columns(4, R, b.K2, A)
        else:
            transpose_into(b.MEM, R)
            grad_columns(4, R, b.V2, 2 * A)
            transpose_into(b.E4, S)
            grad_columns(4, S, b.O2, 3 * A)

    def when(condition, *steps):
        @pl.when(condition)
        def _():
            for step in steps:
                step()

    def ffn_back(i, carry):
        mine = enc_mine(i)
        dy = across_take(sum2, i)
        when(i >= 2, lambda: across_start(sum3, i - 2))
        dz = norm_back(1, dy, b.XH1, b.RS1, i, ROW_FFN_OUT_BIAS)
        b.RES[i] = dz
        gather_start(at.E2, b.E2, mine, i, dz.astype(BF16))
        when(i >= 1, lambda: across_prepare(sum3, i - 1))
        when(i == 0, lambda: grad_step(2, 1))
        when(i == 1, lambda: grad_step(5, 1))
        when(i == 2, lambda: grad_step(0, 2))
        gather_copy(at.E2, b.E2, mine, i).wait()
        rows = enc_rows(i)
        pair_send(sum3, i, feed_back(rows, b.E2[rows, :], b.GP0))
        when(i == 1, lambda: decoder_self_grad(1), lambda: grad_step(7, 0))
        when(i == 2, lambda: grad_step(3, 2), lambda: grad_step(4, 1))
        return carry

    def ffn_back_rest():
        across_start(sum3, 2)
        across_send(sum3, 3)

    def decoder_part(i):
        rows = dec_chunk(i)
        return (
            mm(b.QD[rows, :], b.ATI[3]) + mm(b.KD[rows, :], b.ATI[4]) + mm(b.VD[rows, :], b.ATI[5])
        )

    def decoder_self_back():
        for i in range(2):
            mine = dec_mine(i)
            dy = b.RESD[i] + across_take(dsum4, i)
            dz = norm_back(2, dy, b.XH2, b.RS2, i, ROW_ATT_OUT_BIAS + 1)
            b.RESD[i] = dz
            gather_start(at.E3, b.E3, mine, i, dz.astype(BF16))
        for i in range(2):
            gather_copy(at.E3, b.E3, dec_mine(i), i).wait()
        b.UPD[...] = mm_nt(b.E3[...], b.ATO[1]).astype(BF16)
        attention_back(b.UPD, b.QD, b.OD, jnp.int32(0), b.KD, b.VTD, b.PD, b.QD, S, S)
        b.KD[...] = mm_tn(b.DS[: heads * S, :S], b.QS[: heads * S, :]).astype(BF16)
        b.VD[...] = mm_tn(b.PD[...], b.DOS[: heads * S, :]).astype(BF16)
        pair_send(dsum5, 1 - x, decoder_part(1 - x))
        part = decoder_part(x)
        across_send(dsum5, 1 - x)
        pair_send(dsum5, x, part)
        att_bias(1, b.QD, b.VD)
        outs.dec_grad[...] = b.RESD[x] + pair_take(dsum5, x)

    def decoder_self_grad(half):
        if half == 0:
            transpose_into(b.DX, S)
            grad_columns(6, S, b.QD, 0)
            grad_columns(6, S, b.KD, A)
        else:
            transpose_into(b.DX, S)
            grad_columns(6, S, b.VD, 2 * A)
            transpose_into(b.E3, S)
            grad_columns(6, S, b.OD, 3 * A)

    def encoder_ffn_out_grad():
        transpose_into(b.E2, R)
        grad_columns(8, R, b.ACT0, 0)

    def encoder_ffn_in_grad():
        transpose_into(b.H1, R)
        grad_columns(10, R, b.GP0, 0)

    steps = [pair, across] + [(flipped(dp, bit), t) for bit in (1, 2, 4)]

    def total_copy(buffer, got, first, step):
        return remote(buffer, got.at[step], at.sum, first + step, steps[step])

    def total_step(buffer, got, first, step):
        if not p.inside:
            return
        if step > 0:
            total_copy(buffer, got, first, step - 1).wait()
            buffer[...] += got[step - 1]
        if step < len(steps):
            total_copy(buffer, got, first, step).start()

    def early_step(step):
        total_step(b.SUM, b.SUMR if p.inside else None, 0, step)

    def late_step(step):
        total_step(b.LATE, b.LATR if p.inside else None, 5, step)

    def early_rows():
        ffn_in_bias(0, b.GP0)
        doubled = lax.broadcasted_iota(jnp.int32, (SUM_ROWS, 1), 0) < ROW_FFN_IN_BIAS
        b.SUM[...] = b.SUM[...] * jnp.where(doubled, 0.5, 1.0)

    def att_back(i, carry):
        mine = enc_mine(i)
        slot = lax.rem(i, jnp.int32(2))
        dy = b.RES[i] + across_take(sum3, i)
        dz = norm_back(0, dy, b.XH0, b.RS0, i, ROW_ATT_OUT_BIAS)
        b.RES[i] = dz
        gather_start(at.E1, b.MEM, mine, i, dz.astype(BF16))
        when(i == 0, lambda: early_step(0))
        when(
            i == 2,
            lambda: grad_step(9, 1),
            lambda: early_step(1),
            lambda: grad_step(8, 0),
            lambda: grad_step(2, 2),
            lambda: grad_step(5, 2),
        )
        when(i == 3, lambda: grad_step(11, 1), lambda: grad_step(7, 1))
        gather_copy(at.E1, b.MEM, mine, i).wait()
        rows = enc_rows(i)
        b.UP[rows, :] = mm_nt(b.MEM[rows, :], b.ATO[0]).astype(BF16)
        p_load(i).wait()
        p_ref = b.BIG.at[slot]
        attention_back(b.UP, b.Q, b.O, i * CE, b.K, b.VT, p_ref, b.Q, CE, R)
        for j in range(2):
            cols = slice(2 * j * CE, 2 * (j + 1) * CE)
            b.DK[:, cols] += mm_tn(b.QS[...], b.DS[:, cols])
            b.DV[:, cols] += mm_tn(b.DOS[...], b.BIG[slot, :, cols])
        when(i < 2, lambda: p_load(i + 2).start())
        return carry

    def att_back_rest():
        for j in range(4):
            cols = slice(j * CE, (j + 1) * CE)
            b.K[cols, :] = b.DK[:, cols].astype(BF16).T
            b.V[cols, :] = b.DV[:, cols].astype(BF16).T
        att_bias(0, b.Q, b.V)
        norm_rows = lax.broadcasted_iota(jnp.int32, (LATE_ROWS, 1), 0) < LATE_NORM_ROWS
        b.LATE[...] = b.LATE[...] * jnp.where(norm_rows, 0.5, 1.0)

    def encoder_self_grad(half):
        if half == 0:
            transpose_into(b.X, R)
            grad_columns(12, R, b.Q, 0)
            grad_columns(12, R, b.K, A)
        else:
            transpose_into(b.X, R)
            grad_columns(12, R, b.V, 2 * A)
            transpose_into(b.MEM, R)
            grad_columns(12, R, b.O, 3 * A)

    def encoder_part(turn):
        i = 2 * (1 - x) + turn if turn < 2 else 2 * x + turn - 2
        rows = enc_rows(i)
        part = mm(b.Q[rows, :], b.ATI[0]) + mm(b.K[rows, :], b.ATI[1]) + mm(b.V[rows, :], b.ATI[2])
        pair_send(sum4, i, part)
        if turn < 2:
            across_send(sum4, i)
        else:
            own = (turn - 2) * HE
            outs.enc_grad[own : own + HE, :] = b.RES[i] + pair_take(sum4, i)

    def decoder_last():
        dsum5[1](1 - x).wait_send()
        dsum5[1](x).wait_recv()
        outs.dec_grad[...] += dsum5[6][x].astype(F32)

    def encoder_last(half):
        sum4[1](2 * (1 - x) + half).wait_send()
        sum4[1](2 * x + half).wait_recv()
        own = half * HE
        outs.enc_grad[own : own + HE, :] += sum4[6][2 * x + half].astype(F32)

    decoder_ffn_out_grad()
    grad_step(0, 0)
    grad_step(1, 0)
    decoder_ffn_in_grad()
    grad_step(3, 0)
    grad_step(2, 0)
    cross_back()
    send_two(dsum4, 0, 1, query_part)
    grad_step(1, 1)
    grad_step(0, 1)
    cross_grad(0)
    grad_step(4, 0)
    send_two(sum2, 0, 1, memory_part)
    send_two(sum2, 2, 3, memory_part)
    cross_grad(1)
    grad_step(5, 0)
    decoder_self_back()
    decoder_self_grad(0)
    grad_step(1, 2)
    grad_step(6, 0)
    grad_step(3, 1)
    for copy in load_ffn(0):
        copy.wait()
    lax.fori_loop(0, 4, ffn_back, 0)
    encoder_ffn_out_grad()
    grad_step(9, 0)
    ffn_back_rest()
    grad_step(4, 2)
    grad_step(0, 3)
    grad_step(1, 3)
    encoder_ffn_in_grad()
    grad_step(11, 0)
    grad_step(10, 0)
    grad_step(6, 1)
    early_rows()
    p_load(0).start()
    p_load(1).start()
    b.DK[...] = jnp.zeros((A, R), F32)
    b.DV[...] = jnp.zeros((A, R), F32)
    lax.fori_loop(0, 4, att_back, 0)
    att_back_rest()
    grad_step(9, 2)
    early_step(2)
    grad_step(8, 1)
    grad_step(6, 2)
    grad_step(3, 3)
    grad_step(2, 3)
    encoder_self_grad(0)
    encoder_self_grad(1)
    grad_step(13, 0)
    grad_step(7, 2)
    early_step(3)
    grad_step(5, 3)
    grad_step(12, 0)
    grad_step(11, 2)
    late_step(0)
    encoder_part(0)
    encoder_part(1)
    grad_step(9, 3)
    grad_step(13, 1)
    grad_step(7, 3)
    late_step(1)
    grad_step(6, 3)
    early_step(4)
    grad_step(10, 1)
    grad_step(12, 1)
    late_step(2)
    grad_step(13, 2)
    late_step(3)
    grad_step(10, 2)
    encoder_part(2)
    encoder_part(3)
    encoder_last(0)
    encoder_last(1)
    grad_step(8, 2)
    grad_step(12, 2)
    late_step(4)
    decoder_last()
    grad_step(11, 3)
    grad_step(12, 3)
    grad_step(13, 3)
    grad_step(10, 3)
    grad_step(8, 3)
    early_step(5)
    grad_step(4, 3)
    late_step(5)
    outs.sums[...] = b.SUM[...]
    outs.late[...] = b.LATE[...]
    for copy in ag_x + ag_p + ag_f:
        copy.wait_send()


BIG_RESULTS = 7


def finish(p, counts, *refs):
    D, A, F = p.D, p.A, p.F
    n = BIG_RESULTS
    sources, (sums, late) = refs[:n], refs[n : n + 2]
    targets, small, sems = refs[n + 2 : 2 * n + 2], refs[2 * n + 2 : -1], refs[-1]
    copies = [pltpu.make_async_copy(sources[k], targets[k], sems.at[k]) for k in range(n)]
    for copy in copies:
        copy.start()
    att_in_bias, att_out_bias, ffn_in_bias, ffn_out_bias, gain, shift, rms = small
    att_in_bias[:2, :] = late[LATE_NORM_ROWS : LATE_NORM_ROWS + 2, :]
    att_in_bias[2:, :] = sums[ROW_ATT_IN_BIAS + 2 : ROW_ATT_IN_BIAS + 6, :]
    for owner in range(4):
        for f in range(2):
            row = ROW_FFN_IN_BIAS + 4 * f + owner
            ffn_in_bias[f : f + 1, owner * F : (owner + 1) * F] = sums[row : row + 1, :]
    att_out_bias[...] = sums[ROW_ATT_OUT_BIAS : ROW_ATT_OUT_BIAS + 3, :]
    ffn_out_bias[...] = sums[ROW_FFN_OUT_BIAS : ROW_FFN_OUT_BIAS + 2, :]
    gain[...] = sums[ROW_GAIN : ROW_GAIN + 5, :]
    shift[...] = sums[ROW_SHIFT : ROW_SHIFT + 5, :]
    for row, target in enumerate((att_out_bias, gain, shift)):
        target[0:1, :] = late[row : row + 1, :]
    values = jnp.zeros((1, 128), F32)
    lane = lax.broadcasted_iota(jnp.int32, (1, 128), 1)
    for k, count in enumerate(counts):
        row = sums[ROW_SQUARE + k : ROW_SQUARE + k + 1, :]
        values = jnp.where(lane == k, jnp.sum(row, axis=1, keepdims=True) * (1.0 / count), values)
    rms[...] = jnp.sqrt(values)[0, : len(counts)]
    for copy in copies:
        copy.wait()


def body(n_dp, *args):
    named = Inputs(*args)
    named = named._replace(
        att_in=jnp.transpose(named.att_in, (0, 2, 1)),
        att_out=jnp.transpose(named.att_out, (0, 2, 1)),
        retrieval=jnp.transpose(named.retrieval, (0, 2, 1, 3)),
    )
    p = Plan(named, n_dp)
    D, A, F = p.D, p.A, p.F
    shapes = Outputs(
        dec_output=((p.HD, D), BF16),
        enc_grad=((p.CE, D), F32),
        dec_grad=((p.HD, D), F32),
        sums=((SUM_ROWS, D), F32),
        late=((LATE_ROWS, D), F32),
        probs=((4, p.heads * p.CE, p.R), BF16),
    )
    if p.inside:
        shapes = shapes._replace(
            att_in=((9, p.block, A), F32),
            att_out=((3, p.block, A), F32),
            ffn_in=((2, p.block, F), F32),
            ffn_out=((2, p.block, F), F32),
        )
    else:
        shapes = shapes._replace(grads=((7, 8, p.block, D), BF16))
    hbm = pl.BlockSpec(memory_space=pl.ANY)
    vmem = pl.BlockSpec(memory_space=pltpu.VMEM)
    places, made_shapes, out_specs = [], [], []
    for position, value in enumerate(shapes):
        if value is None:
            places.append(None)
            continue
        places.append(len(made_shapes))
        made_shapes.append(jax.ShapeDtypeStruct(*value))
        out_specs.append(hbm if Outputs._fields[position] in (PROBS, ALL_GRADS) else vmem)
    results = pl.pallas_call(
        functools.partial(kernel, p, places),
        out_shape=made_shapes,
        in_specs=[hbm if fetched else vmem for fetched in IN_HBM],
        out_specs=out_specs,
        scratch_shapes=[
            *p.scratch.values(),
            pltpu.SemaphoreType.DMA((p.n_sems,)),
            pltpu.SemaphoreType.REGULAR((3 * len(GRADS),)),
        ],
        compiler_params=pltpu.CompilerParams(
            collective_id=0, has_side_effects=True, vmem_limit_bytes=67_000_000
        ),
    )(*named)
    made = Outputs(*[None if place is None else results[place] for place in places])
    sums, late = made.sums, made.late
    if not p.inside:
        sums, late = lax.psum((sums, late), (DP, TENSOR))
        whole = made.grads.reshape(7, D, D).astype(F32)
        parts = lax.psum_scatter(whole, DP, scatter_dimension=1, tiled=True)
        found = {grad: parts[k] for k, grad in enumerate(WHOLE)}
        att = [found[ATT, a] for a in range(3)]
        made = made._replace(
            att_in=jnp.stack([att[a][:, j * A : (j + 1) * A] for a in range(3) for j in range(3)]),
            att_out=jnp.stack([att[a][:, 3 * A : 4 * A] for a in range(3)]),
            ffn_in=jnp.stack([found[FFN_IN, f] for f in range(2)]),
            ffn_out=jnp.stack([found[FFN_OUT, f] for f in range(2)]),
        )
    devices = lax.axis_size(DP) * lax.axis_size(TENSOR)
    enc_count = 1.0 * p.CE * devices * D
    dec_count = 1.0 * p.HD * devices * D
    counts = (enc_count, enc_count, dec_count, dec_count, dec_count, enc_count, dec_count)
    large = (
        made.dec_output,
        made.enc_grad,
        made.dec_grad,
        made.att_in,
        made.att_out,
        made.ffn_in,
        made.ffn_out,
    )
    small = ((6, D), (3, D), (2, 4 * F), (2, D), (5, D), (5, D), (7,))
    done = pl.pallas_call(
        functools.partial(finish, p, counts),
        out_shape=[jax.ShapeDtypeStruct(value.shape, value.dtype) for value in large]
        + [jax.ShapeDtypeStruct(shape, F32) for shape in small],
        in_specs=[vmem] * (BIG_RESULTS + 2),
        out_specs=[hbm] * BIG_RESULTS + [vmem] * len(small),
        scratch_shapes=[pltpu.SemaphoreType.DMA((BIG_RESULTS,))],
    )(*large, sums, late)
    dec_output, enc_grad, dec_grad, att_in, att_out, ffn_in, ffn_out = done[:BIG_RESULTS]
    att_in_bias, att_out_bias, ffn_in_bias, ffn_out_bias, gain, shift, rms = done[BIG_RESULTS:]
    return (
        dec_output,
        enc_grad,
        dec_grad,
        att_in,
        att_in_bias,
        att_out,
        att_out_bias,
        ffn_in,
        ffn_in_bias,
        ffn_out,
        ffn_out_bias,
        gain,
        shift,
        rms,
    )


def solution(mesh):
    rows = P((DP, TENSOR), None)
    placed = (
        rows,
        rows,
        P(DP, None),
        P(DP, None, TENSOR, None),
        P(None, None, TENSOR),
        P(None, TENSOR),
        P(None, None, TENSOR),
        P(),
        P(None, None, TENSOR),
        P(None, TENSOR),
        P(None, None, TENSOR),
        P(),
        P(),
        P(),
        rows,
    )
    split = P(None, DP, TENSOR)
    return jax.shard_map(
        functools.partial(body, mesh.shape[DP]),
        mesh=mesh,
        in_specs=placed,
        out_specs=(rows, rows, rows, split, P(), split, P(), split, P(), split, P(), P(), P(), P()),
        check_vma=False,
    )
```
